256 devices in a mesh: dom: 64 (over z, y, core), batch: 4 (over x).
Axes of the slice: x: 4, y: 4, z: 8, core: 2. Of those that a mesh axis runs over, the one named last changes fastest.
Arguments:
- signal: bfloat16 [32768, 4, 4, 256], P('dom', 'batch'), may hold values from -6 to 6
- cotangent: bfloat16 [32768, 4, 3, 256], P('dom', 'batch'), may hold values from -6 to 6
- conv_weight: bfloat16 [2, 2, 256, 256], replicated, may hold values from -0.25 to 0.25
- mix_weight: bfloat16 [3, 256, 256], replicated, may hold values from -0.21875 to 0.21875
- send_rows: int32 [4096, 2], P('dom'), may hold values from 0 to 511
- send_mask: int32 [4096, 2], P('dom'), may hold values 0 or 1
- tile_vals: bfloat16 [1024, 128, 128], P('dom'), may hold values from -0.26953125 to 0.26953125
- tile_row: int32 [1024], P('dom'), may hold values from 0 to 3
- tile_col: int32 [1024], P('dom'), may hold values from 0 to 5
- tile_mask: int32 [1024], P('dom'), may hold values 0 or 1
- hub_owner: int32 [8], replicated, may hold values from 0 to 63, as said below
- hub_rows: int32 [8, 16], replicated, may hold values from 0 to 511
Outputs:
- layer_out: bfloat16 [32768, 4, 3, 256], P('dom', 'batch')
- signal_grad: bfloat16 [32768, 4, 4, 256], P('dom', 'batch')
- conv_grad: float32 [2, 2, 256, 256], replicated
- mix_grad: float32 [3, 256, 256], replicated
The draws below stay inside these ranges and needn't reach their ends.
Inputs may be any that keep to these rules, and one draw needn't show every extreme that they name: `hub_owner`: each owner slot names a different partition.
All inputs are finite; a program needn't handle non-finite values. No bound on the sum of `send_mask` or of `tile_mask` on one device may be relied on, other than what follows from the above.
Results may differ from the reference program's by a relative error of at most 0.0056.
Values may be sent and summed in bfloat16 or wider, within the bound.
No kernel may reach another device: no remote copies, remote signals or barrier semaphores. Data moves between devices by JAX's collectives and lax.ppermute only.
A program may use at most 128 MiB of HBM per device.

```python
import math
import jax
import jax.numpy as jnp
from jax import lax

C = 256
HIST = 4
NODE_DEV = 512
BLK = 128
OWNERS = 8
HUB_PER = 16
T1 = 3
TILES = 16
CAP = 2
HALO = 128
EXT = 768
NODES = 32768
BATCH = 4
N_DOM = 64


def draw_hub_owner(key, part):
    inner_key = jax.random.fold_in(key, 11)
    order_key = jax.random.fold_in(key, 23)
    middle = jax.random.permutation(inner_key, N_DOM - 2)[:OWNERS - 2].astype(jnp.int32) + 1
    ends = jnp.array([0, N_DOM - 1], dtype=jnp.int32)
    owners = jnp.concatenate([ends, middle], 0)
    order = jax.random.permutation(order_key, OWNERS)
    return owners[order].astype(jnp.int32)


def set_ends(drawn, rng, low, high):
    longest = drawn.shape.index(max(drawn.shape))
    spots = []
    for shift in (0, 1):
        where = [jax.random.randint(jax.random.fold_in(rng, axis), (), 0, length) for axis, length in enumerate(drawn.shape)]
        where[longest] = (where[longest] + shift) % drawn.shape[longest]
        spots.append(tuple(where))
    return drawn.at[spots[0]].set(low).at[spots[1]].set(high)


def levels(key, dims, split, smallest, largest):
    factor_of = 1.0
    for position, parts in split:
        draws = jax.random.uniform(jax.random.fold_in(jax.random.fold_in(key, 6), position), (parts,), jnp.float32, smallest / len(split), largest / len(split))
        factor_of = factor_of * jnp.repeat(jnp.exp(draws), dims[position] // parts).reshape((-1,) + (1,) * (len(dims) - 1 - position))
    return factor_of


def gaussian(stream_key, dims, deviation, bound, pieces=(), held_as=jnp.bfloat16):
    values = jax.random.normal(stream_key, dims, jnp.float32) * deviation
    if len(pieces) > 0:
        values = levels(stream_key, dims, pieces, -0.22, 0.18) * values
    return jnp.clip(values, min=-bound, max=bound).astype(held_as)


def setup_inputs(seed: int = 0) -> dict:
    splits = jax.random.split(jax.random.key(seed), 13)
    signal = gaussian(splits[0], (NODES, BATCH, HIST, C), 1.0, 6.0, ((0, 64), (1, 4)))
    cotangent = gaussian(splits[1], (NODES, BATCH, T1, C), 1.0, 6.0, ((0, 64), (1, 4)))
    conv_weight = gaussian(splits[2], (2, 2, C, C), (2 * C) ** -0.5, 0.25)
    mix_weight = gaussian(splits[3], (3, C, C), (3 * C) ** -0.5, 0.21875)
    send_rows = set_ends(jax.random.randint(splits[4], (N_DOM * N_DOM, CAP), 0, NODE_DEV), jax.random.fold_in(splits[4], 1), 0, NODE_DEV - 1).astype(jnp.int32)
    send_mask = set_ends((jax.random.randint(splits[5], (N_DOM * N_DOM, CAP), 0, 3) < 2).astype(jnp.int32), jax.random.fold_in(splits[5], 1), 0, 1)
    tile_vals = gaussian(splits[6], (N_DOM * TILES, BLK, BLK), 0.045, 0.26953125, ((0, 64),))
    tile_row = set_ends(jax.random.randint(splits[7], (N_DOM * TILES,), 0, NODE_DEV // BLK), jax.random.fold_in(splits[7], 1), 0, (NODE_DEV // BLK) - 1).astype(jnp.int32)
    tile_col = set_ends(jax.random.randint(splits[8], (N_DOM * TILES,), 0, EXT // BLK), jax.random.fold_in(splits[8], 1), 0, (EXT // BLK) - 1).astype(jnp.int32)
    tile_mask = set_ends((jax.random.randint(splits[9], (N_DOM * TILES,), 0, 4) < 3).astype(jnp.int32), jax.random.fold_in(splits[9], 1), 0, 1)
    hub_owner = draw_hub_owner(jax.random.fold_in(splits[12], 71), 0)
    hub_rows = set_ends(jax.random.randint(splits[11], (OWNERS, HUB_PER), 0, NODE_DEV), jax.random.fold_in(splits[11], 1), 0, NODE_DEV - 1).astype(jnp.int32)
    return dict(signal=signal, cotangent=cotangent, conv_weight=conv_weight, mix_weight=mix_weight, send_rows=send_rows, send_mask=send_mask, tile_vals=tile_vals, tile_row=tile_row, tile_col=tile_col, tile_mask=tile_mask, hub_owner=hub_owner, hub_rows=hub_rows)


highest = lax.Precision.HIGHEST

def tile_apply(ext_rows, tile_block, row_ids, col_ids, tile_keep, row_tiles):
    block_rows = tile_block.shape[1]
    features = ext_rows.shape[1]
    chosen = ext_rows.reshape(-1, block_rows, features)[col_ids]
    product = jnp.einsum('tij,tjf->tif', tile_block.astype(jnp.float32), chosen.astype(jnp.float32), precision=highest)
    product = product * tile_keep.astype(jnp.float32)[:, None, None]
    onehot = (row_ids[None, :] == jnp.arange(row_tiles, dtype=jnp.int32)[:, None]).astype(jnp.float32)
    return jnp.einsum('rt,tif->rif', onehot, product, precision=highest).reshape(row_tiles * block_rows, features)

def tile_back(own_rows, tile_block, row_ids, col_ids, tile_keep, col_tiles):
    block_rows = tile_block.shape[1]
    features = own_rows.shape[1]
    chosen = own_rows.reshape(-1, block_rows, features)[row_ids]
    product = jnp.einsum('tji,tjf->tif', tile_block.astype(jnp.float32), chosen.astype(jnp.float32), precision=highest)
    product = product * tile_keep.astype(jnp.float32)[:, None, None]
    onehot = (col_ids[None, :] == jnp.arange(col_tiles, dtype=jnp.int32)[:, None]).astype(jnp.float32)
    return jnp.einsum('ct,tif->cif', onehot, product, precision=highest).reshape(col_tiles * block_rows, features)

def device_graph(graph, device):
    send_rows, send_mask, tile_vals, tile_row, tile_col, tile_mask, hub_owner, hub_rows = graph
    sources = lax.dynamic_index_in_dim(send_rows.reshape(N_DOM, N_DOM, CAP), device, 1, keepdims=False)
    source_keep = lax.dynamic_index_in_dim(send_mask.reshape(N_DOM, N_DOM, CAP), device, 1, keepdims=False)
    halo_index = (jnp.arange(N_DOM, dtype=jnp.int32)[:, None] * NODE_DEV + sources).reshape(-1).astype(jnp.int32)
    start = (device * TILES).astype(jnp.int32)
    tiles = (lax.dynamic_slice_in_dim(tile_vals, start, TILES, 0), lax.dynamic_slice_in_dim(tile_row, start, TILES, 0), lax.dynamic_slice_in_dim(tile_col, start, TILES, 0), lax.dynamic_slice_in_dim(tile_mask, start, TILES, 0))
    return (halo_index, source_keep.reshape(-1), tiles)

def hub_index_of(graph):
    hub_owner, hub_rows = (graph[6], graph[7])
    return (hub_owner[:, None] * NODE_DEV + hub_rows).reshape(-1).astype(jnp.int32)

def spread(field, graph):
    hub_index = hub_index_of(graph)
    hubs = field[hub_index]

    def per_device(device):
        halo_index, halo_keep, tiles = device_graph(graph, device)
        own = lax.dynamic_slice_in_dim(field, (device * NODE_DEV).astype(jnp.int32), NODE_DEV, 0)
        halo = field[halo_index] * halo_keep.astype(field.dtype)[:, None]
        ext_rows = jnp.concatenate([own, halo, hubs], 0)
        return tile_apply(ext_rows, tiles[0], tiles[1], tiles[2], tiles[3], NODE_DEV // BLK)
    return lax.map(per_device, jnp.arange(N_DOM, dtype=jnp.int32)).reshape(NODES, -1)

def gather_back(field, graph):
    hub_index = hub_index_of(graph)

    def per_device(carry, device):
        halo_index, halo_keep, tiles = device_graph(graph, device)
        start = (device * NODE_DEV).astype(jnp.int32)
        own = lax.dynamic_slice_in_dim(field, start, NODE_DEV, 0)
        ext_grad = tile_back(own, tiles[0], tiles[1], tiles[2], tiles[3], EXT // BLK)
        block = lax.dynamic_slice_in_dim(carry, start, NODE_DEV, 0) + ext_grad[:NODE_DEV]
        carry = lax.dynamic_update_slice_in_dim(carry, block, start, 0)
        carry = carry.at[halo_index].add(ext_grad[NODE_DEV:NODE_DEV + HALO] * halo_keep.astype(jnp.float32)[:, None])
        carry = carry.at[hub_index].add(ext_grad[NODE_DEV + HALO:])
        return (carry, None)
    total, unused = lax.scan(per_device, jnp.zeros(field.shape, jnp.float32), jnp.arange(N_DOM, dtype=jnp.int32))
    return total

def mm(left, right):
    return jnp.dot(left, right, preferred_element_type=jnp.float32)

def one_sample(signal_s, grad_s, conv_weight, mix_weight, graph):
    earlier = signal_s[:, :-1, :].reshape(-1, C)
    later = signal_s[:, 1:, :].reshape(-1, C)
    filt = mm(earlier, conv_weight[0, 0]) + mm(later, conv_weight[0, 1])
    gate = mm(earlier, conv_weight[1, 0]) + mm(later, conv_weight[1, 1])
    tanh_filt = jnp.tanh(filt)
    sig_gate = jax.nn.sigmoid(gate)
    hidden = (tanh_filt * sig_gate).astype(jnp.bfloat16)
    hop_one = spread(hidden.reshape(NODES, T1 * C), graph).astype(jnp.bfloat16).reshape(-1, C)
    hop_two = spread(hop_one.reshape(NODES, T1 * C), graph).astype(jnp.bfloat16).reshape(-1, C)
    mixed = later.astype(jnp.float32) + mm(hidden, mix_weight[0]) + mm(hop_one, mix_weight[1]) + mm(hop_two, mix_weight[2])
    layer_out = mixed.astype(jnp.bfloat16).reshape(NODES, T1, C)
    grad_out = grad_s.reshape(-1, C)
    mix_part = jnp.stack([mm(hidden.T, grad_out), mm(hop_one.T, grad_out), mm(hop_two.T, grad_out)])
    back_two = mm(grad_out, mix_weight[2].T).astype(jnp.bfloat16)
    back_one = mm(grad_out, mix_weight[1].T) + gather_back(back_two.reshape(NODES, T1 * C), graph).reshape(-1, C)
    back_one = back_one.astype(jnp.bfloat16)
    grad_hidden = mm(grad_out, mix_weight[0].T) + gather_back(back_one.reshape(NODES, T1 * C), graph).reshape(-1, C)
    grad_filt = (grad_hidden * sig_gate * (1.0 - tanh_filt * tanh_filt)).astype(jnp.bfloat16)
    grad_gate = (grad_hidden * tanh_filt * sig_gate * (1.0 - sig_gate)).astype(jnp.bfloat16)
    conv_part = jnp.stack([jnp.stack([mm(earlier.T, grad_filt), mm(later.T, grad_filt)]), jnp.stack([mm(earlier.T, grad_gate), mm(later.T, grad_gate)])])
    into_earlier = (mm(grad_filt, conv_weight[0, 0].T) + mm(grad_gate, conv_weight[1, 0].T)).reshape(NODES, T1, C)
    into_later = (mm(grad_filt, conv_weight[0, 1].T) + mm(grad_gate, conv_weight[1, 1].T) + grad_out.astype(jnp.float32)).reshape(NODES, T1, C)
    signal_grad = jnp.pad(into_earlier, ((0, 0), (0, 1), (0, 0))) + jnp.pad(into_later, ((0, 0), (1, 0), (0, 0)))
    return (layer_out, signal_grad.astype(jnp.bfloat16), conv_part, mix_part)

def reference(signal, cotangent, conv_weight, mix_weight, send_rows, send_mask, tile_vals, tile_row, tile_col, tile_mask, hub_owner, hub_rows):
    graph = (send_rows, send_mask, tile_vals, tile_row, tile_col, tile_mask, hub_owner, hub_rows)

    def per_sample(sample_pair):
        return one_sample(sample_pair[0], sample_pair[1], conv_weight, mix_weight, graph)
    outs, grads, conv_parts, mix_parts = lax.map(per_sample, (jnp.moveaxis(signal, 1, 0), jnp.moveaxis(cotangent, 1, 0)))
    factor = 1.0 / math.sqrt(NODES * BATCH * T1)
    return (jnp.moveaxis(outs, 0, 1), jnp.moveaxis(grads, 0, 1), lax.optimization_barrier(jnp.sum(conv_parts, 0)) * factor, lax.optimization_barrier(jnp.sum(mix_parts, 0)) * factor)
```

```python
import math

import jax
import jax.numpy as jnp
from jax import lax
from jax.experimental import pallas as pl
from jax.experimental.pallas import tpu as pltpu
from jax.sharding import PartitionSpec as P

BF = jnp.bfloat16
F32 = jnp.float32
I32 = jnp.int32
NODE = 512
EXT = 768
BLK = 128
C = 256
T1 = 3
HIST = 4
DOM = 64
BATCH = 4
LIMIT = 50 * 1024 * 1024


def nn(a, b):
    return jnp.dot(a, b, preferred_element_type=F32)


def nt(a, b):
    return lax.dot_general(a, b, (((1,), (1,)), ((), ())), preferred_element_type=F32)


def tn(a, b):
    return lax.dot_general(a, b, (((0,), (0,)), ((), ())), preferred_element_type=F32)


def iota(shape, dim):
    return lax.broadcasted_iota(I32, shape, dim)


def hot(mask):
    return jnp.where(mask, 1.0, 0.0).astype(BF)


def pick_rows(column, count):
    return hot(column == iota((column.shape[0], count), 1))


def put_rows(row, count):
    return hot(row == iota((count, row.shape[1]), 0))


def gates(early, late, conv):
    filt = nn(early, conv[0, 0]) + nn(late, conv[0, 1])
    gate = nn(early, conv[1, 0]) + nn(late, conv[1, 1])
    th = jnp.tanh(filt)
    sg = jax.nn.sigmoid(gate)
    return (th * sg).astype(BF), sg * (1.0 - th * th), th * sg * (1.0 - sg)


def start_kernel(
    trow, tcol, tmask, sig, cot, tiles, cols, a_ref, at_ref, eown, ehub, send, acc
):
    acc[...] = jnp.zeros_like(acc)

    def add(i, carry):
        at = trow[i] * 6 + tcol[i]
        acc[at] += tiles[i].astype(F32) * tmask[i].astype(F32)
        return carry

    lax.fori_loop(0, tiles.shape[0], add, 0)
    for r in range(4):
        for c in range(6):
            block = acc[r * 6 + c]
            a_ref[r * BLK : (r + 1) * BLK, c * BLK : (c + 1) * BLK] = block.astype(BF)
            at_ref[c * BLK : (c + 1) * BLK, r * BLK : (r + 1) * BLK] = block.T.astype(BF)
    pick_sig = pick_rows(cols[:, 0:1], NODE)
    pick_ext = pick_rows(cols[:, 1:2], EXT - NODE)
    for t in range(T1):
        ext = nn(at_ref[...], cot[t])
        eown[t] = ext[:NODE]
        ehub[t] = ext[NODE + BLK :]
        last = pick_rows(cols[:, 2 + t : 3 + t], NODE)
        out = (
            nn(pick_sig, sig[t])
            + nn(last, sig[HIST - 1])
            + nn(pick_ext, ext[NODE:].astype(BF))
        )
        send[:, t * C : (t + 1) * C] = out.astype(BF)


def own_kernel(sig, cot, conv, mix, a_ref, hid, fac_f, fac_g, hop, gw, mix0):
    total = jnp.zeros((C, C), F32)
    for t in range(T1):
        h, p, q = gates(sig[t], sig[t + 1], conv)
        hid[t] = h
        fac_f[t] = p
        fac_g[t] = q
        hop[t] = nn(a_ref[:, :NODE], h)
        gw[t] = nt(cot[t], mix[0])
        total += tn(h, cot[t])
    mix0[...] = total


def hub_blocks(recv, owner, with_last):
    row = iota((8, NODE), 0)
    m = iota((8, NODE), 1)
    which = row >> 2
    step = row & 3
    forward = jnp.zeros((8, C), F32)
    backward = jnp.zeros((8, C), F32)
    for c in range(T1):
        block = recv[:, c * C : (c + 1) * C]
        f = (step == c) & (m == owner * 8 + 2 + which)
        if with_last and c == 2:
            f = f | ((row == 3) & (m == owner * 8 + 6))
        if with_last and c == 0:
            f = f | ((row == 7) & (m == owner * 8 + 7))
        b = (step == c) & ((m & 7) == 2 + which) & ((m >> 3) != owner)
        forward += nn(hot(f), block)
        backward += nn(hot(b), block)
    return forward, backward


def hub_kernel(scal, recv, send):
    owner = scal[0]
    forward, backward = hub_blocks(recv, owner, True)
    at_owner = iota((DOM, 8, C), 0) == owner
    send[...] = jnp.where(at_owner, backward[None], forward[None]).astype(BF)


def middle_kernel(
    recv1, recv2, sig, cot, conv, mix, a_ref, at_ref, eown, ehub, hid, fac_f, fac_g,
    hop_part, gw, mix0, cols, rows, hubcol, hubrow, send, wsend, hop_out, gh_out, ehub2,
):
    halo = BLK
    r = iota((halo, NODE), 0)
    m = iota((halo, NODE), 1)
    base = (r >> 1) * 8
    odd = r & 1
    pick0 = hot(m == base + odd)
    pick3a = hot((odd == 0) & (m == base + 6))
    pick3b = hot((odd == 1) & (m == base + 6))
    own_node = hubcol[:, 0:1]
    own_pick = pick_rows(own_node, NODE)
    ext_sig = []
    for t in range(HIST):
        if t < T1:
            rows_halo = nn(pick0, recv1[:, t * C : (t + 1) * C])
        else:
            rows_halo = nn(pick3a, recv1[:, 0:C]) + nn(pick3b, recv1[:, C : 2 * C])
        hub_pick = hot((m == base + odd * 4 + t) & (own_node < 0))
        rows_hub = nn(hub_pick, recv2[...]) + nn(own_pick, sig[t])
        ext_sig.append(jnp.concatenate([rows_halo, rows_hub], 0).astype(BF))
    put_halo = put_rows(rows[0:1, :], NODE)
    put_hub_own = put_rows(hubrow[0:1, :], NODE)
    pick_sig = pick_rows(cols[:, 0:1], NODE)
    pick_ext = pick_rows(cols[:, 1:2], EXT - NODE)
    column = iota((NODE, NODE), 1)
    node = iota((NODE, NODE), 0)
    grads = [[jnp.zeros((C, C), F32) for _ in range(2)] for _ in range(2)]
    mix1 = jnp.zeros((C, C), F32)
    mix2 = jnp.zeros((C, C), F32)
    for t in range(T1):
        h, p, q = gates(ext_sig[t], ext_sig[t + 1], conv)
        hop = (hop_part[t] + nn(a_ref[:, NODE:], h)).astype(BF)
        hop_out[t] = hop
        put_hub = hot((rows[1:2, :] == node) & ((column & 3) == t))
        back = (
            eown[t]
            + nn(put_halo, recv1[:, t * C : (t + 1) * C])
            + nn(put_hub, recv2[...])
            + nn(put_hub_own, ehub[t].astype(BF))
        ).astype(BF)
        mix1 += tn(hop, cot[t])
        mix2 += tn(hop, back)
        ext = nn(at_ref[...], back)
        ehub2[t] = ext[NODE + BLK :]
        ext = ext.astype(BF)
        out = nn(pick_sig, hop) + nn(pick_ext, ext[NODE:])
        send[:, t * C : (t + 1) * C] = out.astype(BF)
        through = nt(ext, mix[2])
        gh = gw[t] + nt(back, mix[1]) + through[:NODE]
        gh_out[t] = gh
        far = through[NODE:]
        own = ((gh * fac_f[t]).astype(BF), (gh * fac_g[t]).astype(BF))
        other = ((far * p).astype(BF), (far * q).astype(BF))
        for k in range(2):
            for s in range(2):
                grads[k][s] += tn(sig[t + s], own[k]) + tn(ext_sig[t + s], other[k])
    parts = [grads[0][0], grads[0][1], grads[1][0], grads[1][1], mix0[...], mix1, mix2]
    for k, part in enumerate(parts):
        wsend[k * C : (k + 1) * C, :] = part.astype(BF)
    wsend[7 * C :, :] = jnp.zeros((C, C), BF)


def join_kernel(rows, parts, send):
    send[:, : T1 * C] = rows[...]
    total = parts[0].astype(F32)
    for b in range(1, BATCH):
        total += parts[b].astype(F32)
    send[:, T1 * C :] = total.astype(BF)


def hub_weight_kernel(scal, recv, send):
    owner = scal[0]
    forward, backward = hub_blocks(recv, owner, False)
    row = iota((8, NODE), 0)
    m = iota((8, NODE), 1)
    weights = nn(hot((m & 7) == row), recv[:, T1 * C :])
    at_owner = iota((DOM, 16, C), 0) == owner
    to_others = jnp.concatenate([forward, weights], 0)
    to_owner = jnp.concatenate([backward, weights], 0)
    send[...] = jnp.where(at_owner, to_owner[None], to_others[None]).astype(BF)


def end_kernel(
    recv3, recv4, sig, cot, conv, mix, a_ref, hid, fac_f, fac_g, hop_ref, gh_ref, ehub2,
    rows, rows4, hubcol, hubrow, layer, sgrad,
):
    halo = BLK
    r = iota((halo, NODE), 0)
    m = iota((halo, NODE), 1)
    pick0 = hot(m == (r >> 1) * 8 + (r & 1))
    r4 = iota((halo, 2 * NODE), 0)
    m4 = iota((halo, 2 * NODE), 1)
    base4 = (r4 >> 1) * 16 + (r4 & 1) * 4
    own_node = hubcol[:, 0:1]
    own_pick = pick_rows(own_node, NODE)
    put_halo = put_rows(rows[0:1, :], NODE)
    put_hub_own = put_rows(hubrow[0:1, :], NODE)
    column4 = iota((NODE, 2 * NODE), 1)
    node4 = iota((NODE, 2 * NODE), 0)
    for t in range(T1):
        block = recv3[:, t * C : (t + 1) * C]
        hop = hop_ref[t]
        hub_pick = hot((m4 == base4 + t) & (own_node < 0))
        rows_halo = nn(pick0, block).astype(BF)
        rows_hub = (nn(hub_pick, recv4[...]) + nn(own_pick, hop)).astype(BF)
        two = (
            nn(a_ref[:, :NODE], hop)
            + nn(a_ref[:, NODE : NODE + BLK], rows_halo)
            + nn(a_ref[:, NODE + BLK :], rows_hub)
        ).astype(BF)
        mixed = (
            sig[t + 1].astype(F32) + nn(hid[t], mix[0]) + nn(hop, mix[1]) + nn(two, mix[2])
        )
        layer[t] = mixed.astype(BF)
        put_hub = hot((rows4[0:1, :] == node4) & ((column4 & 3) == t))
        back = (
            nn(put_halo, block)
            + nn(put_hub, recv4[...])
            + nn(put_hub_own, ehub2[t].astype(BF))
        ).astype(BF)
        gh = gh_ref[t] + nt(back, mix[2])
        gf = (gh * fac_f[t]).astype(BF)
        gg = (gh * fac_g[t]).astype(BF)
        early = nt(gf, conv[0, 0]) + nt(gg, conv[1, 0])
        late = nt(gf, conv[0, 1]) + nt(gg, conv[1, 1]) + cot[t].astype(F32)
        if t == 0:
            sgrad[0] = early.astype(BF)
        else:
            sgrad[t] = (early + carried).astype(BF)
        carried = late
    sgrad[T1] = carried.astype(BF)


VM = pl.BlockSpec(memory_space=pltpu.VMEM)
SM = pl.BlockSpec(memory_space=pltpu.SMEM)


def call(kernel, outs, args, smem=0, scratch=(), flops=0):
    return pl.pallas_call(
        kernel,
        out_shape=[jax.ShapeDtypeStruct(s, d) for s, d in outs],
        in_specs=[SM] * smem + [VM] * (len(args) - smem),
        out_specs=[VM] * len(outs),
        scratch_shapes=list(scratch),
        compiler_params=pltpu.CompilerParams(vmem_limit_bytes=LIMIT),
        cost_estimate=pl.CostEstimate(flops=flops, bytes_accessed=8 << 20, transcendentals=0),
    )(*args)


def swap(x, axis):
    return lax.all_to_all(x, axis, split_axis=0, concat_axis=0, tiled=True)


def body(
    signal,
    cotangent,
    conv,
    mix,
    send_rows,
    send_mask,
    tile_vals,
    tile_row,
    tile_col,
    tile_mask,
    hub_owner,
    hub_rows,
):
    me = lax.axis_index("dom").astype(I32)
    sig = jnp.transpose(signal[:, 0], (1, 0, 2))
    cot = jnp.transpose(cotangent[:, 0], (1, 0, 2))

    part = jnp.arange(DOM, dtype=I32)
    none = jnp.full((DOM, 1), -1, I32)
    none2 = jnp.full((DOM, 2), -1, I32)
    used = jnp.where(send_mask == 1, send_rows, -1)
    mine = (jnp.repeat(hub_owner, 8) == me)[:, None]
    own_hub = jnp.where(mine, hub_rows.reshape(DOM, 2), -1)
    two = 2 * part[:, None] + jnp.arange(2, dtype=I32)[None]
    pick_sig = jnp.concatenate([used, own_hub, none2, none2], 1)
    pick_ext = jnp.concatenate([none2, jnp.where(mine, -1, BLK + two), two, none2], 1)
    six = jnp.full((DOM, 6), -1, I32)
    last0 = jnp.concatenate([six, used[:, 0:1], own_hub[:, 1:2]], 1)
    last1 = jnp.concatenate([six, used[:, 1:2], none], 1)
    last2 = jnp.concatenate([six, own_hub[:, 0:1], none], 1)
    cols = jnp.stack([pick_sig, pick_ext, last0, last1, last2], -1).reshape(NODE, 5)
    back_row = jnp.concatenate([none2, none2, used, none2], 1).reshape(1, NODE)
    hub_back = jnp.repeat(own_hub, 4, axis=1)
    rows = jnp.concatenate([back_row, hub_back.reshape(1, NODE)], 0)
    rows4 = jnp.concatenate([hub_back, jnp.full((DOM, 8), -1, I32)], 1).reshape(1, 2 * NODE)
    hubcol = own_hub.reshape(BLK, 1)
    hubrow = own_hub.reshape(1, BLK)
    scal = hub_owner[me // 8].reshape(1)

    field = (T1, NODE, C)
    a_mat, at_mat, eown, ehub, send1 = call(
        start_kernel,
        [((NODE, EXT), BF), ((EXT, NODE), BF), (field, F32), ((T1, BLK, C), F32), ((NODE, EXT), BF)],
        (tile_row, tile_col, tile_mask, sig, cot, tile_vals, cols),
        smem=3,
        scratch=[pltpu.VMEM((24, BLK, BLK), F32)],
        flops=2 << 30,
    )
    recv1 = swap(send1.reshape(DOM, 8, EXT), "dom").reshape(NODE, EXT)
    hid, fac_f, fac_g, hop_part, gw, mix0 = call(
        own_kernel,
        [(field, BF), (field, F32), (field, F32), (field, F32), (field, F32), ((C, C), F32)],
        (sig, cot, conv, mix, a_mat),
        flops=3 << 30,
    )
    (send2,) = call(hub_kernel, [((DOM, 8, C), BF)], (scal, recv1), smem=1, flops=1 << 28)
    recv2 = swap(send2, "dom").reshape(NODE, C)
    send3, wsend, hop, gh, ehub2 = call(
        middle_kernel,
        [
            ((NODE, EXT), BF),
            ((8 * C, C), BF),
            (field, BF),
            (field, F32),
            ((T1, BLK, C), F32),
        ],
        (recv1, recv2, sig, cot, conv, mix, a_mat, at_mat, eown, ehub, hid, fac_f, fac_g,
         hop_part, gw, mix0, cols, rows, hubcol, hubrow),
        flops=8 << 30,
    )
    wrecv = swap(wsend.reshape(BATCH, NODE, C), "batch")
    (send3w,) = call(join_kernel, [((NODE, 4 * C), BF)], (send3, wrecv), flops=1 << 28)
    recv3 = swap(send3w.reshape(DOM, 8, 4 * C), "dom").reshape(NODE, 4 * C)
    (send4,) = call(hub_weight_kernel, [((DOM, 16, C), BF)], (scal, recv3), smem=1, flops=1 << 28)
    recv4 = swap(send4, "dom")
    mine4 = recv4[:, 8:].reshape(NODE, C)
    whole = swap(jnp.broadcast_to(mine4[None], (BATCH, NODE, C)), "batch").reshape(8 * C, C)
    layer, sgrad = call(
        end_kernel,
        [(field, BF), ((HIST, NODE, C), BF)],
        (recv3, recv4.reshape(2 * NODE, C), sig, cot, conv, mix, a_mat, hid, fac_f, fac_g, hop,
         gh, ehub2, rows, rows4, hubcol, hubrow),
        flops=6 << 30,
    )
    factor = 1.0 / math.sqrt(NODE * DOM * BATCH * T1)
    whole = whole.astype(F32) * factor
    return (
        jnp.transpose(layer, (1, 0, 2))[:, None],
        jnp.transpose(sgrad, (1, 0, 2))[:, None],
        whole[: 4 * C].reshape(2, 2, C, C),
        whole[4 * C : 7 * C].reshape(3, C, C),
    )


def solution(mesh):
    placed = (
        P("dom", "batch", None, None),
        P("dom", "batch", None, None),
        P(),
        P(),
        P("dom", None),
        P("dom", None),
        P("dom", None, None),
        P("dom"),
        P("dom"),
        P("dom"),
        P(),
        P(),
    )
    return jax.shard_map(
        body,
        mesh=mesh,
        in_specs=placed,
        out_specs=(P("dom", "batch", None, None), P("dom", "batch", None, None), P(), P()),
        check_vma=False,
    )
```

```python
import math

import jax
import jax.numpy as jnp
from jax import lax
from jax.experimental import pallas as pl
from jax.experimental.pallas import tpu as pltpu
from jax.sharding import PartitionSpec as P

BF = jnp.bfloat16
F32 = jnp.float32
I32 = jnp.int32
NODE = 512
EXT = 768
BLK = 128
C = 256
T1 = 3
HIST = 4
DOM = 64
BATCH = 4
OWNERS = 8
HUB_PER = 16
TILES = 16


def nn(a, b):
    return jnp.dot(a, b, preferred_element_type=F32)


def nt(a, b):
    return lax.dot_general(a, b, (((1,), (1,)), ((), ())), preferred_element_type=F32)


def tn(a, b):
    return lax.dot_general(a, b, (((0,), (0,)), ((), ())), preferred_element_type=F32)


def iota(shape, dim):
    return lax.broadcasted_iota(I32, shape, dim)


def hot(mask):
    return jnp.where(mask, 1.0, 0.0).astype(BF)


def pick_rows(column, count):
    return hot(column == iota((column.shape[0], count), 1))


def put_rows(row, count):
    return hot(row == iota((count, row.shape[1]), 0))


def gates(early, late, conv):
    filt = nn(early, conv[0, 0]) + nn(late, conv[0, 1])
    gate = nn(early, conv[1, 0]) + nn(late, conv[1, 1])
    th = jnp.tanh(filt)
    sg = jax.nn.sigmoid(gate)
    return (th * sg).astype(BF), sg * (1.0 - th * th), th * sg * (1.0 - sg)


def call(kernel, outs, args, mib=60, smem=0, scratch=(), flops=0):
    vmem = pl.BlockSpec(memory_space=pltpu.VMEM)
    return pl.pallas_call(
        kernel,
        out_shape=[jax.ShapeDtypeStruct(s, d) for s, d in outs],
        in_specs=[pl.BlockSpec(memory_space=pltpu.SMEM)] * smem + [vmem] * (len(args) - smem),
        out_specs=[vmem] * len(outs),
        scratch_shapes=list(scratch),
        compiler_params=pltpu.CompilerParams(vmem_limit_bytes=mib << 20),
        cost_estimate=pl.CostEstimate(flops=flops, bytes_accessed=8 << 20, transcendentals=0),
    )(*args)


def high_low(x):
    return (x >> 4).astype(F32).astype(BF), (x & 15).astype(F32).astype(BF)


def start_kernel(
    trow, tcol, tmask, me, owners, tiles, used_rows, used_mask, hubs, cot, sig,
    a_out, a_hub, at_out, cols_out, rows_out, send, acc,
):
    slot = jnp.int32(-1)
    for o in range(OWNERS):
        slot = jnp.where(owners[o] == me[0], o, slot)
    used = jnp.where(used_mask[...] == 1, used_rows[...] + 1, 0)
    held = jnp.where(iota((OWNERS, HUB_PER), 0) == slot, hubs[...] + 1, 0)
    held = jnp.broadcast_to(jnp.sum(held, 0, keepdims=True), (8, HUB_PER))
    held_high, held_low = high_low(held)
    j16 = iota((HUB_PER, DOM), 0)
    q16 = iota((HUB_PER, DOM), 1)
    line = iota((8, DOM), 0)
    values = jnp.where(line == 0, used[0:1], jnp.where(line == 1, used[1:2], 0))
    for i in range(2):
        lay = hot((j16 == 2 * (q16 & 7) + i) & ((q16 >> 3) == slot))
        wide = (16.0 * nn(held_high, lay) + nn(held_low, lay)).astype(I32)
        values = jnp.where(line == 2 + i, wide, values)
    high, low = high_low(values)

    def down(count, shift):
        pick = hot((iota((count, DOM), 0) >> shift) == iota((count, DOM), 1))
        return (16.0 * nt(pick, high) + nt(pick, low)).astype(I32) - 1

    def along(count, shift):
        pick = hot((iota((DOM, count), 1) >> shift) == iota((DOM, count), 0))
        return (16.0 * nn(high, pick) + nn(low, pick)).astype(I32) - 1

    by_row = down(NODE, 3)
    m = iota((NODE, 1), 0)
    j = m & 7
    first, second, hub0, hub1 = [by_row[:, k : k + 1] for k in range(4)]
    pick_sig = jnp.where(j == 0, first, jnp.where(j == 1, second, -1))
    pick_sig = jnp.where(j == 2, hub0, jnp.where(j == 3, hub1, pick_sig))
    two = 2 * (m >> 3) + (j & 1)
    not_mine = (m >> 6) != slot
    pick_ext = jnp.where((j >> 1) == 2, two, -1)
    pick_ext = jnp.where(((j >> 1) == 1) & not_mine, BLK + two, pick_ext)
    last = [
        jnp.where(j == 6, first, jnp.where(j == 7, hub1, -1)),
        jnp.where(j == 6, second, -1),
        jnp.where(j == 6, hub0, -1),
    ]
    by_hub = down(BLK, 1)
    odd = (iota((BLK, 1), 0) & 1) == 1
    hub_col = jnp.where(odd, by_hub[:, 3:4], by_hub[:, 2:3])
    lane = iota((NODE, BLK), 1)
    hub_wide = jnp.concatenate([hub_col, jnp.full((NODE - BLK, 1), -1, I32)], 0)
    cols_out[...] = jnp.where(
        lane == 0, pick_sig, jnp.where(lane == 1, pick_ext, jnp.where(lane == 2, hub_wide, -1))
    )
    flat = along(NODE, 3)
    mr = iota((1, NODE), 1)
    jr = mr & 7
    back_row = jnp.where(jr == 4, flat[0:1], jnp.where(jr == 5, flat[1:2], -1))
    hub_back = jnp.where(((mr >> 2) & 1) == 0, flat[2:3], flat[3:4])
    flat_hub = along(BLK, 1)
    odd = (iota((1, BLK), 1) & 1) == 1
    hub_row = jnp.where(odd, flat_hub[3:4], flat_hub[2:3])
    hub_row = jnp.concatenate([hub_row, jnp.full((1, NODE - BLK), -1, I32)], 1)
    line = iota((8, NODE), 0)
    rows_out[...] = jnp.where(
        line == 0, back_row, jnp.where(line == 1, hub_back, jnp.where(line == 2, hub_row, -1))
    )

    acc[...] = jnp.zeros_like(acc)
    tile = tiles

    def add(i, carry):
        at = trow[i] * 6 + tcol[i]
        acc[at] += tile[i].astype(F32) * tmask[i].astype(F32)
        return carry

    lax.fori_loop(0, TILES, add, 0)
    for r in range(4):
        for c in range(6):
            block = acc[r * 6 + c]
            a_out[r * BLK : (r + 1) * BLK, c * BLK : (c + 1) * BLK] = block.astype(BF)
            at_out[c * BLK : (c + 1) * BLK, r * BLK : (r + 1) * BLK] = block.T.astype(BF)
    a_hub[...] = a_out[:, NODE + BLK :]
    from_sig = pick_rows(pick_sig, NODE)
    from_ext = pick_rows(pick_ext, EXT - NODE)
    for t in range(T1):
        ext = nn(at_out[NODE:, :], cot[t]).astype(BF)
        out = (
            nn(from_ext, ext)
            + nn(from_sig, sig[t])
            + nn(pick_rows(last[t], NODE), sig[HIST - 1])
        )
        send[:, t * C : (t + 1) * C] = out.astype(BF)


def own_kernel(conv, sig, cot, hid, fac_f, fac_g, mix0):
    total = jnp.zeros((C, C), F32)
    weights = conv
    for t in range(T1):
        h, p, q = gates(sig[t], sig[t + 1], weights)
        hid[t] = h
        fac_f[t] = p
        fac_g[t] = q
        total += tn(h, cot[t])
    mix0[...] = total


def hub_blocks(recv, owner, with_last):
    row = iota((8, NODE), 0)
    m = iota((8, NODE), 1)
    which = row >> 2
    step = row & 3
    forward = jnp.zeros((8, C), F32)
    backward = jnp.zeros((8, C), F32)
    for c in range(T1):
        block = recv[:, c * C : (c + 1) * C]
        f = (step == c) & (m == owner * 8 + 2 + which)
        if with_last and c == 2:
            f = f | ((row == 3) & (m == owner * 8 + 6))
        if with_last and c == 0:
            f = f | ((row == 7) & (m == owner * 8 + 7))
        b = (step == c) & ((m & 7) == 2 + which) & ((m >> 3) != owner)
        forward += nn(hot(f), block)
        backward += nn(hot(b), block)
    return forward, backward


def hub_kernel(me, owners, recv, send):
    owner = owners[me[0] >> 3]
    forward, backward = hub_blocks(recv, owner, True)
    at_owner = iota((DOM, 8, C), 0) == owner
    send[...] = jnp.where(at_owner, backward[None], forward[None]).astype(BF)


def halo_kernel(
    recv, conv, cols, rows, at_mat, a_mat, hid, cot, sig, back, hop, sig_x, hub_sig
):
    r = iota((BLK, NODE), 0)
    m = iota((BLK, NODE), 1)
    base = (r >> 1) * 8
    odd = r & 1
    pick0 = hot(m == base + odd)
    pick3a = hot((odd == 0) & (m == base + 6))
    pick3b = hot((odd == 1) & (m == base + 6))
    blocks = [recv[:, t * C : (t + 1) * C] for t in range(T1)]
    weights = conv
    far = [nn(pick0, block).astype(BF) for block in blocks]
    far.append((nn(pick3a, blocks[0]) + nn(pick3b, blocks[1])).astype(BF))
    for t in range(HIST):
        sig_x[t] = far[t]
    hid_x = [gates(far[t], far[t + 1], weights)[0] for t in range(T1)]
    put_halo = put_rows(rows[0:1, :], NODE)
    put_hub_own = put_rows(rows[2:3, 0:BLK], NODE)
    for t in range(T1):
        hub = nn(at_mat[NODE + BLK :, :], cot[t]).astype(BF)
        back[t] = (
            nn(at_mat[:NODE, :], cot[t]) + nn(put_halo, blocks[t]) + nn(put_hub_own, hub)
        )
        hop[t] = nn(a_mat[:, :NODE], hid[t]) + nn(a_mat[:, NODE : NODE + BLK], hid_x[t])
    own_pick = pick_rows(cols[0:BLK, 2:3], NODE)
    for t in range(HIST):
        hub_sig[t] = nn(own_pick, sig[t]).astype(BF)


def rows_kernel(
    recv, cols, rows, conv, hub_sig, a_hub, hop_part, back_part, at_mat,
    send, back_out, hop_out, ext_out, ext_hub, sig_x,
):
    r = iota((BLK, NODE), 0)
    m = iota((BLK, NODE), 1)
    base = (r >> 1) * 8 + (r & 1) * 4
    own_node = cols[0:BLK, 2:3]
    hubs = recv[...]
    far = []
    for t in range(HIST):
        hub_pick = hot((m == base + t) & (own_node < 0))
        far.append((nn(hub_pick, hubs) + hub_sig[t].astype(F32)).astype(BF))
        sig_x[t] = far[t]
    pick_sig = pick_rows(cols[:, 0:1], NODE)
    pick_ext = pick_rows(cols[:, 1:2], EXT - NODE)
    column = iota((NODE, NODE), 1)
    node = iota((NODE, NODE), 0)
    weights = conv
    for t in range(T1):
        h = gates(far[t], far[t + 1], weights)[0]
        hop = (hop_part[t] + nn(a_hub[...], h)).astype(BF)
        hop_out[t] = hop
        put_hub = hot((rows[1:2, :] == node) & ((column & 3) == t))
        back = (back_part[t] + nn(put_hub, hubs)).astype(BF)
        back_out[t] = back
        ext = nn(at_mat[...], back).astype(BF)
        out = nn(pick_sig, hop) + nn(pick_ext, ext[NODE:])
        send[:, t * C : (t + 1) * C] = out.astype(BF)
        ext_out[t] = ext
        ext_hub[t] = ext[NODE + BLK :]


def weight_kernel(
    core, conv, mix, hop, cot, back, ext, sig, sig_h, sig_u, fac_f, fac_g, mix0,
    keep, give, gh_out,
):
    grads = [[jnp.zeros((C, C), F32) for _ in range(2)] for _ in range(2)]
    mix1 = jnp.zeros((C, C), F32)
    mix2 = jnp.zeros((C, C), F32)
    weights = conv
    far_sig = [None] * HIST

    def far_at(t):
        if far_sig[t] is None:
            far_sig[t] = jnp.concatenate([sig_h[t], sig_u[t]], 0)
        return far_sig[t]

    for t in range(T1):
        mix1 += tn(hop[t], cot[t])
        mix2 += tn(hop[t], back[t])
        through = nt(ext[t], mix[2])
        gh = nt(cot[t], mix[0]) + nt(back[t], mix[1]) + through[:NODE]
        gh_out[t] = gh
        _, p, q = gates(far_at(t), far_at(t + 1), weights)
        own = ((gh * fac_f[t]).astype(BF), (gh * fac_g[t]).astype(BF))
        far = ((through[NODE:] * p).astype(BF), (through[NODE:] * q).astype(BF))
        for s in range(2):
            for k in range(2):
                grads[k][s] += tn(sig[t + s], own[k]) + tn(far_at(t + s), far[k])
    low = [grads[0][0], grads[0][1], grads[1][0], grads[1][1]]
    high = [mix0[...], mix1, mix2, jnp.zeros((C, C), F32)]
    first = core[0] == 0
    for k in range(4):
        stay = jnp.where(first, low[k], high[k])
        away = jnp.where(first, high[k], low[k])
        for s in range(2):
            at = (2 * k + s) * C
            give[at : at + C, :] = away[:, s * BLK : (s + 1) * BLK]
            keep[at : at + C, :] = stay[:, s * BLK : (s + 1) * BLK]


def pair_kernel(batch, keep, got, *outs):
    mine, other = keep, got
    for k in range(BATCH):
        at = pl.ds(pl.multiple_of(((batch[0] + k) & (BATCH - 1)) * NODE, NODE), NODE)
        outs[k][...] = (mine[at, :] + other[at, :]).astype(BF)


def second_hub_kernel(me, owners, recv, part0, part1, part2, part3, send):
    owner = owners[me[0] >> 3]
    forward, backward = hub_blocks(recv, owner, False)
    total = part0[...].astype(F32) + part1[...].astype(F32)
    total += part2[...].astype(F32) + part3[...].astype(F32)
    at_owner = iota((DOM, 8, C), 0) == owner
    send[:, :, 0:C] = jnp.where(at_owner, backward[None], forward[None]).astype(BF)
    send[:, :, C:] = total.astype(BF).reshape(DOM, 8, BLK)


def spread_kernel(recv, send):
    even = jnp.zeros((8, BLK), F32)
    odd = jnp.zeros((8, BLK), F32)
    for p in range(0, DOM, 2):
        even += recv[p, :, C:].astype(F32)
        odd += recv[p + 1, :, C:].astype(F32)
    is_odd = (iota((DOM, 8, BLK), 0) & 1) == 1
    send[...] = jnp.where(is_odd, odd[None], even[None]).astype(BF)


def near_kernel(
    recv, cols, rows, a_mat, mix, hop_ref, hid, sig, ext_hub, gh_ref, mixed, two, gh_out, hop_hub
):
    r = iota((BLK, NODE), 0)
    m = iota((BLK, NODE), 1)
    pick0 = hot(m == (r >> 1) * 8 + (r & 1))
    own_pick = pick_rows(cols[0:BLK, 2:3], NODE)
    put_halo = put_rows(rows[0:1, :], NODE)
    put_hub_own = put_rows(rows[2:3, 0:BLK], NODE)
    for t in range(T1):
        block = recv[:, t * C : (t + 1) * C]
        hop = hop_ref[t]
        rows_halo = nn(pick0, block).astype(BF)
        two[t] = nn(a_mat[:, :NODE], hop) + nn(a_mat[:, NODE : NODE + BLK], rows_halo)
        hop_hub[t] = nn(own_pick, hop).astype(BF)
        mixed[t] = sig[t + 1].astype(F32) + nn(hid[t], mix[0]) + nn(hop, mix[1])
        back = (nn(put_halo, block) + nn(put_hub_own, ext_hub[t])).astype(BF)
        gh_out[t] = gh_ref[t] + nt(back, mix[2])


def end_kernel(
    recv, cols, rows, a_hub, mix, conv, hop_hub, mixed, two_ref, gh_ref, fac_f, fac_g, cot,
    layer, sgrad,
):
    r = iota((BLK, NODE), 0)
    m = iota((BLK, NODE), 1)
    base = (r >> 1) * 8 + (r & 1) * 4
    own_node = cols[0:BLK, 2:3]
    column = iota((NODE, NODE), 1)
    node = iota((NODE, NODE), 0)
    hubs = recv[:, 0:C]
    for t in range(T1):
        hub_pick = hot((m == base + t) & (own_node < 0))
        rows_hub = (nn(hub_pick, hubs) + hop_hub[t].astype(F32)).astype(BF)
        two = (two_ref[t] + nn(a_hub[...], rows_hub)).astype(BF)
        layer[t] = (mixed[t] + nn(two, mix[2])).astype(BF)
        put_hub = hot((rows[1:2, :] == node) & ((column & 3) == t))
        gh = gh_ref[t] + nt(nn(put_hub, hubs).astype(BF), mix[2])
        gf = (gh * fac_f[t]).astype(BF)
        gg = (gh * fac_g[t]).astype(BF)
        early = nt(gf, conv[0, 0]) + nt(gg, conv[1, 0])
        late = nt(gf, conv[0, 1]) + nt(gg, conv[1, 1]) + cot[t].astype(F32)
        if t == 0:
            sgrad[0] = early.astype(BF)
        else:
            sgrad[t] = (early + carried).astype(BF)
        carried = late
    sgrad[T1] = carried.astype(BF)


def scale_kernel(core, batch, *refs):
    mine, other = refs[0:BATCH], refs[BATCH : 2 * BATCH]
    conv_grad, mix_grad = refs[2 * BATCH :]
    factor = 1.0 / math.sqrt(NODE * DOM * BATCH * T1)
    first = core[0] == 0
    for k in range(BATCH):
        block = (batch[0] + BATCH - k) & (BATCH - 1)
        for s in range(2):
            one = mine[k][s * C : (s + 1) * C, :].astype(F32) * factor
            two = other[k][s * C : (s + 1) * C, :].astype(F32) * factor
            lanes = slice(s * BLK, (s + 1) * BLK)
            conv_grad[block, :, lanes] = jnp.where(first, one, two)

            @pl.when(block < 3)
            def _():
                mix_grad[block, :, lanes] = jnp.where(first, two, one)


def swap(x, axis):
    return lax.all_to_all(x, axis, split_axis=0, concat_axis=0, tiled=True)


def body(
    signal,
    cotangent,
    conv,
    mix,
    send_rows,
    send_mask,
    tile_vals,
    tile_row,
    tile_col,
    tile_mask,
    hub_owner,
    hub_rows,
):
    me = lax.axis_index("dom").astype(I32)
    core = (me & 1).reshape(1)
    me = me.reshape(1)
    batch = lax.axis_index("batch").astype(I32).reshape(1)
    sig = jnp.transpose(signal[:, 0], (1, 0, 2))
    cot = jnp.transpose(cotangent[:, 0], (1, 0, 2))

    field = (T1, NODE, C)
    edge = (T1, BLK, C)
    edge4 = (HIST, BLK, C)
    half = (8 * C, BLK)
    chunk = (NODE, BLK)
    a_mat, a_hub, at_mat, cols, rows, send1 = call(
        start_kernel,
        [((NODE, EXT), BF), ((NODE, BLK), BF), ((EXT, NODE), BF), ((NODE, BLK), I32),
         ((8, NODE), I32), ((NODE, EXT), BF)],
        (tile_row, tile_col, tile_mask, me, hub_owner, tile_vals, send_rows.T, send_mask.T,
         hub_rows, cot, sig),
        smem=5,
        scratch=[pltpu.VMEM((24, BLK, BLK), F32)],
        flops=2 << 30,
    )
    recv1 = swap(send1.reshape(DOM, 8, EXT), "dom").reshape(NODE, EXT)
    hid, fac_f, fac_g, mix0 = call(
        own_kernel,
        [(field, BF), (field, F32), (field, F32), ((C, C), F32)],
        (conv, sig, cot),
        flops=8 << 30,
    )
    (send2,) = call(
        hub_kernel, [((DOM, 8, C), BF)], (me, hub_owner, recv1), 8, smem=2, flops=1 << 28
    )
    recv2 = swap(send2, "dom").reshape(NODE, C)
    back_part, hop_part, sig_h, hub_sig = call(
        halo_kernel,
        [(field, F32), (field, F32), (edge4, BF), (edge4, BF)],
        (recv1, conv, cols, rows, at_mat, a_mat, hid, cot, sig),
        flops=8 << 30,
    )
    send3, back, hop, ext, ext_hub, sig_u = call(
        rows_kernel,
        [((NODE, EXT), BF), (field, BF), (field, BF), ((T1, EXT, C), BF), (edge, BF),
         (edge4, BF)],
        (recv2, cols, rows, conv, hub_sig, a_hub, hop_part, back_part, at_mat),
        flops=4 << 30,
    )
    recv3 = swap(send3.reshape(DOM, 8, EXT), "dom").reshape(NODE, EXT)
    keep, give, gh = call(
        weight_kernel,
        [(half, F32), (half, F32), (field, F32)],
        (core, conv, mix, hop, cot, back, ext, sig, sig_h, sig_u, fac_f, fac_g, mix0),
        smem=1,
        flops=8 << 30,
    )
    pairs = [(i, i ^ 1) for i in range(DOM)]
    rounds = [[(i, (i + k) % BATCH) for i in range(BATCH)] for k in range(BATCH)]
    got = lax.ppermute(give, "dom", pairs)
    parts = call(
        pair_kernel, [(chunk, BF)] * BATCH, (batch, keep, got), 8, smem=1, flops=1 << 26
    )
    parts = [parts[0]] + [
        lax.ppermute(parts[k], "batch", rounds[k]) for k in range(1, BATCH)
    ]
    (send4,) = call(
        second_hub_kernel,
        [((DOM, 8, C + BLK), BF)],
        (me, hub_owner, recv3, *parts),
        8,
        smem=2,
        flops=1 << 28,
    )
    recv4 = swap(send4, "dom")
    mixed, two, gh, hop_hub = call(
        near_kernel,
        [(field, F32), (field, F32), (field, F32), (edge, BF)],
        (recv3, cols, rows, a_mat, mix, hop, hid, sig, ext_hub, gh),
        flops=8 << 30,
    )
    recv4, mixed, two, gh, hop_hub = lax.optimization_barrier((recv4, mixed, two, gh, hop_hub))
    (send5,) = call(spread_kernel, [((DOM, 8, BLK), BF)], (recv4,), 6, flops=1 << 26)
    recv5 = swap(send5, "dom").reshape(chunk)
    layer, sgrad = call(
        end_kernel,
        [(field, BF), ((HIST, NODE, C), BF)],
        (recv4.reshape(NODE, C + BLK), cols, rows, a_hub, mix, conv, hop_hub, mixed, two, gh,
         fac_f, fac_g, cot),
        flops=12 << 30,
    )
    layer = jnp.transpose(layer, (1, 0, 2))[:, None]
    sgrad = jnp.transpose(sgrad, (1, 0, 2))[:, None]
    recv5, layer, sgrad = lax.optimization_barrier((recv5, layer, sgrad))
    mine = [recv5] + [lax.ppermute(recv5, "batch", rounds[k]) for k in range(1, BATCH)]
    other = [lax.ppermute(one, "dom", pairs) for one in mine]
    conv_grad, mix_grad = call(
        scale_kernel,
        [((4, C, C), F32), ((3, C, C), F32)],
        (core, batch, *mine, *other),
        10,
        smem=2,
        flops=1 << 20,
    )
    return layer, sgrad, conv_grad.reshape(2, 2, C, C), mix_grad


def solution(mesh):
    placed = (
        P("dom", "batch", None, None),
        P("dom", "batch", None, None),
        P(),
        P(),
        P("dom", None),
        P("dom", None),
        P("dom", None, None),
        P("dom"),
        P("dom"),
        P("dom"),
        P(),
        P(),
    )
    return jax.shard_map(
        body,
        mesh=mesh,
        in_specs=placed,
        out_specs=(P("dom", "batch", None, None), P("dom", "batch", None, None), P(), P()),
        check_vma=False,
    )
```

```python
import math

import jax
import jax.numpy as jnp
from jax import lax
from jax.experimental import pallas as pl
from jax.experimental.pallas import tpu as pltpu
from jax.sharding import PartitionSpec as P

BF = jnp.bfloat16
F32 = jnp.float32
I32 = jnp.int32
NODE = 512
EXT = 768
BLK = 128
C = 256
T1 = 3
HIST = 4
DOM = 64
BATCH = 4
OWNERS = 8
HUB_PER = 16
TILES = 16


def nn(a, b):
    return jnp.dot(a, b, preferred_element_type=F32)


def nt(a, b):
    return lax.dot_general(a, b, (((1,), (1,)), ((), ())), preferred_element_type=F32)


def tn(a, b):
    return lax.dot_general(a, b, (((0,), (0,)), ((), ())), preferred_element_type=F32)


def iota(shape, dim):
    return lax.broadcasted_iota(I32, shape, dim)


def hot(mask):
    return jnp.where(mask, 1.0, 0.0).astype(BF)


def pick_rows(column, count):
    return hot(column == iota((column.shape[0], count), 1))


def put_rows(row, count):
    return hot(row == iota((count, row.shape[1]), 0))


def gates(early, late, conv):
    filt = nn(early, conv[0, 0]) + nn(late, conv[0, 1])
    gate = nn(early, conv[1, 0]) + nn(late, conv[1, 1])
    th = jnp.tanh(filt)
    sg = jax.nn.sigmoid(gate)
    return (th * sg).astype(BF), sg * (1.0 - th * th), th * sg * (1.0 - sg)


def call(kernel, outs, args, mib=60, smem=0, scratch=(), flops=0):
    vmem = pl.BlockSpec(memory_space=pltpu.VMEM)
    return pl.pallas_call(
        kernel,
        out_shape=[jax.ShapeDtypeStruct(s, d) for s, d in outs],
        in_specs=[pl.BlockSpec(memory_space=pltpu.SMEM)] * smem + [vmem] * (len(args) - smem),
        out_specs=[vmem] * len(outs),
        scratch_shapes=list(scratch),
        compiler_params=pltpu.CompilerParams(vmem_limit_bytes=mib << 20),
        cost_estimate=pl.CostEstimate(flops=flops, bytes_accessed=8 << 20, transcendentals=0),
    )(*args)


def stepped(kernel, outs, args, kinds, out_kinds, smem=0, scratch=(), flops=0):
    def spec(shape, kind):
        if kind == "all":
            return pl.BlockSpec(shape, lambda t: (0,) * len(shape))
        if kind == "lanes":
            return pl.BlockSpec((shape[0], C), lambda t: (0, t))
        ahead = 1 if kind == "next" else 0
        return pl.BlockSpec((1,) + shape[1:], lambda t: (t + ahead,) + (0,) * (len(shape) - 1))

    return pl.pallas_call(
        kernel,
        grid=(T1,),
        out_shape=[jax.ShapeDtypeStruct(s, d) for s, d in outs],
        in_specs=[pl.BlockSpec(memory_space=pltpu.SMEM)] * smem
        + [spec(x.shape, k) for x, k in zip(args[smem:], kinds)],
        out_specs=[spec(s, k) for (s, d), k in zip(outs, out_kinds)],
        scratch_shapes=list(scratch),
        compiler_params=pltpu.CompilerParams(vmem_limit_bytes=60 << 20),
        cost_estimate=pl.CostEstimate(flops=flops, bytes_accessed=8 << 20, transcendentals=0),
    )(*args)


def high_low(x):
    return (x >> 4).astype(F32).astype(BF), (x & 15).astype(F32).astype(BF)


def add_tiles(acc, trow, tcol, tmask, tiles, low):
    acc[...] = jnp.zeros_like(acc)

    def add(i, carry):
        @pl.when((tmask[i] == 1) & (tcol[i] >= low))
        def _():
            acc[(tcol[i] - low) * 4 + trow[i]] += tiles[i].astype(F32)

        return carry

    lax.fori_loop(0, TILES, add, 0)


def slot_of(me, owners):
    slot = jnp.int32(-1)
    for o in range(OWNERS):
        slot = jnp.where(owners[o] == me[0], o, slot)
    return slot


def own_hub_block(me, owners, rows, recv):
    at = pl.multiple_of(jnp.maximum(slot_of(me, owners), 0) * DOM, DOM)
    return recv[pl.ds(at, DOM), 0:C], rows[3:4, 0:DOM]


def put_step(target, t):
    at = iota((NODE, DOM), 1)
    return hot((target == iota((NODE, DOM), 0)) & ((at & 3) == t))


def start_kernel(
    trow, tcol, tmask, me, owners, tiles, used_rows, used_mask, hubs, cot, sig,
    cols_out, rows_out, send, acc, far,
):
    slot = slot_of(me, owners)
    used = jnp.where(used_mask[...] == 1, used_rows[...] + 1, 0)
    held = jnp.where(iota((OWNERS, HUB_PER), 0) == slot, hubs[...] + 1, 0)
    held = jnp.broadcast_to(jnp.sum(held, 0, keepdims=True), (8, HUB_PER))
    held_high, held_low = high_low(held)
    j16 = iota((HUB_PER, DOM), 0)
    q16 = iota((HUB_PER, DOM), 1)
    line = iota((8, DOM), 0)
    values = jnp.where(line == 0, used[0:1], jnp.where(line == 1, used[1:2], 0))
    for i in range(2):
        lay = hot((j16 == 2 * (q16 & 7) + i) & ((q16 >> 3) == slot))
        wide = (16.0 * nn(held_high, lay) + nn(held_low, lay)).astype(I32)
        values = jnp.where(line == 2 + i, wide, values)
    high, low = high_low(values)

    def down(count, shift):
        pick = hot((iota((count, DOM), 0) >> shift) == iota((count, DOM), 1))
        return (16.0 * nt(pick, high) + nt(pick, low)).astype(I32) - 1

    def along(count, shift):
        pick = hot((iota((DOM, count), 1) >> shift) == iota((DOM, count), 0))
        return (16.0 * nn(high, pick) + nn(low, pick)).astype(I32) - 1

    by_row = down(NODE, 3)
    m = iota((NODE, 1), 0)
    j = m & 7
    first, second, hub0, hub1 = [by_row[:, k : k + 1] for k in range(4)]
    pick_sig = jnp.where(j == 0, first, jnp.where(j == 1, second, -1))
    pick_sig = jnp.where(j == 2, hub0, jnp.where(j == 3, hub1, pick_sig))
    two = 2 * (m >> 3) + (j & 1)
    not_mine = (m >> 6) != slot
    pick_ext = jnp.where((j >> 1) == 2, two, -1)
    pick_ext = jnp.where(((j >> 1) == 1) & not_mine, BLK + two, pick_ext)
    last = [
        jnp.where(j == 6, first, jnp.where(j == 7, hub1, -1)),
        jnp.where(j == 6, second, -1),
        jnp.where(j == 6, hub0, -1),
    ]
    by_hub = down(BLK, 1)
    odd = (iota((BLK, 1), 0) & 1) == 1
    hub_col = jnp.where(odd, by_hub[:, 3:4], by_hub[:, 2:3])
    lane = iota((NODE, BLK), 1)
    hub_wide = jnp.concatenate([hub_col, jnp.full((NODE - BLK, 1), -1, I32)], 0)
    cols_out[...] = jnp.where(
        lane == 0, pick_sig, jnp.where(lane == 1, pick_ext, jnp.where(lane == 2, hub_wide, -1))
    )
    flat = along(NODE, 3)
    mr = iota((1, NODE), 1)
    jr = mr & 7
    back_row = jnp.where(jr == 4, flat[0:1], jnp.where(jr == 5, flat[1:2], -1))
    flat_hub = along(BLK, 1)
    odd = (iota((1, BLK), 1) & 1) == 1
    hub_row = jnp.where(odd, flat_hub[3:4], flat_hub[2:3])
    hub_row = jnp.concatenate([hub_row, jnp.full((1, NODE - BLK), -1, I32)], 1)
    j16 = iota((HUB_PER, NODE), 0)
    at = iota((HUB_PER, NODE), 1)
    lay = hot((j16 == 2 * (at >> 3) + ((at >> 2) & 1)) & (at < DOM))
    hub_mine = (16.0 * nn(held_high, lay) + nn(held_low, lay)).astype(I32)[0:1] - 1
    line = iota((8, NODE), 0)
    rows_out[...] = jnp.where(
        line == 0, back_row, jnp.where(line == 2, hub_row, jnp.where(line == 3, hub_mine, -1))
    )

    add_tiles(acc, trow, tcol, tmask, tiles, 4)
    for r in range(4):
        for c in range(2):
            block = acc[c * 4 + r]
            far[c * BLK : (c + 1) * BLK, r * BLK : (r + 1) * BLK] = block.T.astype(BF)
    from_sig = pick_rows(pick_sig, NODE)
    from_ext = pick_rows(pick_ext, EXT - NODE)
    for t in range(T1):
        ext = nn(far[...], cot[t]).astype(BF)
        out = (
            nn(from_ext, ext)
            + nn(from_sig, sig[t])
            + nn(pick_rows(last[t], NODE), sig[HIST - 1])
        )
        send[:, t * C : (t + 1) * C] = out.astype(BF)


def own_kernel(
    trow, tcol, tmask, tiles, conv, sig, cot, a_out, a_hub, at_out, hid, fac_f, fac_g, mix0, acc
):
    add_tiles(acc, trow, tcol, tmask, tiles, 0)
    for r in range(4):
        for c in range(6):
            block = acc[c * 4 + r]
            a_out[r * BLK : (r + 1) * BLK, c * BLK : (c + 1) * BLK] = block.astype(BF)
            at_out[c * BLK : (c + 1) * BLK, r * BLK : (r + 1) * BLK] = block.T.astype(BF)
    a_hub[...] = a_out[:, NODE + BLK :]
    total = jnp.zeros((C, C), F32)
    weights = conv
    for t in range(T1):
        h, p, q = gates(sig[t], sig[t + 1], weights)
        hid[t] = h
        fac_f[t] = p
        fac_g[t] = q
        total += tn(h, cot[t])
    mix0[...] = total


def hub_blocks(recv, owner, with_last):
    row = iota((8, NODE), 0)
    m = iota((8, NODE), 1)
    which = row >> 2
    step = row & 3
    forward = jnp.zeros((8, C), F32)
    backward = jnp.zeros((8, C), F32)
    for c in range(T1):
        block = recv[:, c * C : (c + 1) * C]
        f = (step == c) & (m == owner * 8 + 2 + which)
        if with_last and c == 2:
            f = f | ((row == 3) & (m == owner * 8 + 6))
        if with_last and c == 0:
            f = f | ((row == 7) & (m == owner * 8 + 7))
        b = (step == c) & ((m & 7) == 2 + which) & ((m >> 3) != owner)
        forward += nn(hot(f), block)
        backward += nn(hot(b), block)
    return forward, backward


def hub_kernel(me, owners, recv, send):
    owner = owners[me[0] >> 3]
    forward, backward = hub_blocks(recv, owner, True)
    at_owner = iota((DOM, 8, C), 0) == owner
    send[...] = jnp.where(at_owner, backward[None], forward[None]).astype(BF)


def halo_kernel(
    recv, conv, cols, rows, at_mat, a_mat, hid, cot, sig, back, hop, sig_x, hub_sig
):
    r = iota((BLK, NODE), 0)
    m = iota((BLK, NODE), 1)
    base = (r >> 1) * 8
    odd = r & 1
    pick0 = hot(m == base + odd)
    pick3a = hot((odd == 0) & (m == base + 6))
    pick3b = hot((odd == 1) & (m == base + 6))
    blocks = [recv[:, t * C : (t + 1) * C] for t in range(T1)]
    weights = conv
    far = [nn(pick0, block).astype(BF) for block in blocks]
    far.append((nn(pick3a, blocks[0]) + nn(pick3b, blocks[1])).astype(BF))
    for t in range(HIST):
        sig_x[t] = far[t]
    hid_x = [gates(far[t], far[t + 1], weights)[0] for t in range(T1)]
    put_halo = put_rows(rows[0:1, :], NODE)
    put_hub_own = put_rows(rows[2:3, 0:BLK], NODE)
    for t in range(T1):
        hub = nn(at_mat[NODE + BLK :, :], cot[t]).astype(BF)
        back[t] = (
            nn(at_mat[:NODE, :], cot[t]) + nn(put_halo, blocks[t]) + nn(put_hub_own, hub)
        )
        hop[t] = nn(a_mat[:, :NODE], hid[t]) + nn(a_mat[:, NODE : NODE + BLK], hid_x[t])
    own_pick = pick_rows(cols[0:BLK, 2:3], NODE)
    for t in range(HIST):
        hub_sig[t] = nn(own_pick, sig[t]).astype(BF)


def rows_kernel(
    me, owners, recv, cols, rows, conv, hub0, hub1, a_hub, hop_part, back_part, at_mat,
    send, back_out, hop_out, ext_out, ext_hub, sig_x, pick_sig, pick_ext,
):
    t = pl.program_id(0)

    @pl.when(t == 0)
    def _():
        pick_sig[...] = pick_rows(cols[:, 0:1], NODE)
        pick_ext[...] = pick_rows(cols[:, 1:2], EXT - NODE)

    r = iota((BLK, NODE), 0)
    m = iota((BLK, NODE), 1)
    base = (r >> 1) * 8 + (r & 1) * 4
    own_node = cols[0:BLK, 2:3]
    hubs = recv[...]
    far = []
    for s, hub_sig in ((0, hub0), (1, hub1)):
        hub_pick = hot((m == base + (t + s)) & (own_node < 0))
        far.append((nn(hub_pick, hubs) + hub_sig[0].astype(F32)).astype(BF))
        sig_x[t + s] = far[s]
    mine, target = own_hub_block(me, owners, rows, recv)
    h = gates(far[0], far[1], conv)[0]
    hop = (hop_part[0] + nn(a_hub[...], h)).astype(BF)
    hop_out[0] = hop
    back = (back_part[0] + nn(put_step(target, t), mine)).astype(BF)
    back_out[0] = back
    ext = nn(at_mat[...], back).astype(BF)
    out = nn(pick_sig[...], hop) + nn(pick_ext[...], ext[NODE:])
    send[...] = out.astype(BF)
    ext_out[0] = ext
    ext_hub[0] = ext[NODE + BLK :]


def weight_kernel(
    core, conv, mix, hop, cot, back, ext, sig0, sig1, halo0, halo1, hub0, hub1, fac_f, fac_g,
    mix0, keep, give, acc,
):
    t = pl.program_id(0)

    @pl.when(t == 0)
    def _():
        acc[...] = jnp.zeros_like(acc)

    acc[4] += tn(hop[0], cot[0])
    acc[5] += tn(hop[0], back[0])
    through = nt(ext[0], mix[2])
    gh = nt(cot[0], mix[0]) + nt(back[0], mix[1]) + through[:NODE]
    far_sig = (
        jnp.concatenate([halo0[0], hub0[0]], 0),
        jnp.concatenate([halo1[0], hub1[0]], 0),
    )
    _, p, q = gates(far_sig[0], far_sig[1], conv)
    own = ((gh * fac_f[0]).astype(BF), (gh * fac_g[0]).astype(BF))
    far = ((through[NODE:] * p).astype(BF), (through[NODE:] * q).astype(BF))
    for s, sig in ((0, sig0), (1, sig1)):
        for k in range(2):
            acc[2 * k + s] += tn(sig[0], own[k]) + tn(far_sig[s], far[k])

    @pl.when(t == T1 - 1)
    def _():
        first = core[0] == 0
        for k in range(4):
            low = acc[k]
            high = (mix0[...], acc[4], acc[5], jnp.zeros((C, C), F32))[k]
            stay = jnp.where(first, low, high)
            away = jnp.where(first, high, low)
            for s in range(2):
                at = (2 * k + s) * C
                give[at : at + C, :] = away[:, s * BLK : (s + 1) * BLK]
                keep[at : at + C, :] = stay[:, s * BLK : (s + 1) * BLK]


def pair_kernel(batch, keep, got, *outs):
    mine, other = keep, got
    for k in range(BATCH):
        at = pl.ds(pl.multiple_of(((batch[0] + k) & (BATCH - 1)) * NODE, NODE), NODE)
        outs[k][...] = (mine[at, :] + other[at, :]).astype(BF)


def second_hub_kernel(me, owners, recv, part0, part1, part2, part3, send):
    owner = owners[me[0] >> 3]
    forward, backward = hub_blocks(recv, owner, False)
    total = part0[...].astype(F32) + part1[...].astype(F32)
    total += part2[...].astype(F32) + part3[...].astype(F32)
    at_owner = iota((DOM, 8, C), 0) == owner
    send[:, :, 0:C] = jnp.where(at_owner, backward[None], forward[None]).astype(BF)
    send[:, :, C:] = total.astype(BF).reshape(DOM, 8, BLK)


def spread_kernel(recv, send):
    even = jnp.zeros((8, BLK), F32)
    odd = jnp.zeros((8, BLK), F32)
    for p in range(0, DOM, 2):
        even += recv[p, :, C:].astype(F32)
        odd += recv[p + 1, :, C:].astype(F32)
    is_odd = (iota((DOM, 8, BLK), 0) & 1) == 1
    send[...] = jnp.where(is_odd, odd[None], even[None]).astype(BF)


def near_kernel(
    recv, cols, rows, a_mat, mix, hop_ref, hid, sig, ext_hub, ext, back_ref, cot,
    mixed, two, gh_out, hop_hub,
):
    r = iota((BLK, NODE), 0)
    m = iota((BLK, NODE), 1)
    pick0 = hot(m == (r >> 1) * 8 + (r & 1))
    own_pick = pick_rows(cols[0:BLK, 2:3], NODE)
    put_halo = put_rows(rows[0:1, :], NODE)
    put_hub_own = put_rows(rows[2:3, 0:BLK], NODE)
    for t in range(T1):
        block = recv[:, t * C : (t + 1) * C]
        hop = hop_ref[t]
        rows_halo = nn(pick0, block).astype(BF)
        two[t] = nn(a_mat[:, :NODE], hop) + nn(a_mat[:, NODE : NODE + BLK], rows_halo)
        hop_hub[t] = nn(own_pick, hop).astype(BF)
        mixed[t] = sig[t + 1].astype(F32) + nn(hid[t], mix[0]) + nn(hop, mix[1])
        back = (nn(put_halo, block) + nn(put_hub_own, ext_hub[t])).astype(BF)
        own = nt(cot[t], mix[0]) + nt(back_ref[t], mix[1]) + nt(ext[t, 0:NODE, :], mix[2])
        gh_out[t] = own + nt(back, mix[2])


def signal_kernel(
    me, owners, recv, rows, mix, conv, gh_ref, fac_f, fac_g, cot, sgrad
):
    mine, target = own_hub_block(me, owners, rows, recv)
    for t in range(T1):
        back = nn(put_step(target, t), mine).astype(BF)
        gh = gh_ref[t] + nt(back, mix[2])
        gf = (gh * fac_f[t]).astype(BF)
        gg = (gh * fac_g[t]).astype(BF)
        early = nt(gf, conv[0, 0]) + nt(gg, conv[1, 0])
        late = nt(gf, conv[0, 1]) + nt(gg, conv[1, 1]) + cot[t].astype(F32)
        if t == 0:
            sgrad[0] = early.astype(BF)
        else:
            sgrad[t] = (early + carried).astype(BF)
        carried = late
    sgrad[T1] = carried.astype(BF)


def layer_kernel(recv, cols, a_hub, mix, hop_hub, mixed, two_ref, layer):
    r = iota((BLK, NODE), 0)
    m = iota((BLK, NODE), 1)
    base = (r >> 1) * 8 + (r & 1) * 4
    own_node = cols[0:BLK, 2:3]
    hubs = recv[:, 0:C]
    for t in range(T1):
        hub_pick = hot((m == base + t) & (own_node < 0))
        rows_hub = (nn(hub_pick, hubs) + hop_hub[t].astype(F32)).astype(BF)
        two = (two_ref[t] + nn(a_hub[...], rows_hub)).astype(BF)
        layer[t] = (mixed[t] + nn(two, mix[2])).astype(BF)


def tie_kernel(chunk, kept, chunk_out, kept_out):
    del kept, kept_out
    chunk_out[...] = chunk[...]


def scale_kernel(core, batch, *refs):
    mine, other = refs[0:BATCH], refs[BATCH : 2 * BATCH]
    conv_grad, mix_grad = refs[2 * BATCH :]
    factor = 1.0 / math.sqrt(NODE * DOM * BATCH * T1)
    first = core[0] == 0
    for k in range(BATCH):
        block = (batch[0] + BATCH - k) & (BATCH - 1)
        for s in range(2):
            one = mine[k][s * C : (s + 1) * C, :].astype(F32) * factor
            two = other[k][s * C : (s + 1) * C, :].astype(F32) * factor
            lanes = slice(s * BLK, (s + 1) * BLK)
            conv_grad[block, :, lanes] = jnp.where(first, one, two)

            @pl.when(block < 3)
            def _():
                mix_grad[block, :, lanes] = jnp.where(first, two, one)


def swap(x, axis):
    return lax.all_to_all(x, axis, split_axis=0, concat_axis=0, tiled=True)


def body(
    signal,
    cotangent,
    conv,
    mix,
    send_rows,
    send_mask,
    tile_vals,
    tile_row,
    tile_col,
    tile_mask,
    hub_owner,
    hub_rows,
):
    me = lax.axis_index("dom").astype(I32)
    core = (me & 1).reshape(1)
    me = me.reshape(1)
    batch = lax.axis_index("batch").astype(I32).reshape(1)
    sig = jnp.transpose(signal[:, 0], (1, 0, 2))
    cot = jnp.transpose(cotangent[:, 0], (1, 0, 2))

    field = (T1, NODE, C)
    edge = (T1, BLK, C)
    edge4 = (HIST, BLK, C)
    half = (8 * C, BLK)
    chunk = (NODE, BLK)
    cols, rows, send1 = call(
        start_kernel,
        [((NODE, BLK), I32), ((8, NODE), I32), ((NODE, EXT), BF)],
        (tile_row, tile_col, tile_mask, me, hub_owner, tile_vals, send_rows.T, send_mask.T,
         hub_rows, cot, sig),
        smem=5,
        scratch=[pltpu.VMEM((8, BLK, BLK), F32), pltpu.VMEM((EXT - NODE, NODE), BF)],
        flops=2 << 30,
    )
    recv1 = swap(send1.reshape(DOM, 8, EXT), "dom").reshape(NODE, EXT)
    a_mat, a_hub, at_mat, hid, fac_f, fac_g, mix0 = call(
        own_kernel,
        [((NODE, EXT), BF), ((NODE, BLK), BF), ((EXT, NODE), BF), (field, BF), (field, F32),
         (field, F32), ((C, C), F32)],
        (tile_row, tile_col, tile_mask, tile_vals, conv, sig, cot),
        smem=3,
        scratch=[pltpu.VMEM((24, BLK, BLK), F32)],
        flops=8 << 30,
    )
    (send2,) = call(
        hub_kernel, [((DOM, 8, C), BF)], (me, hub_owner, recv1), 8, smem=2, flops=1 << 28
    )
    recv2 = swap(send2, "dom").reshape(NODE, C)
    back_part, hop_part, sig_h, hub_sig = call(
        halo_kernel,
        [(field, F32), (field, F32), (edge4, BF), (edge4, BF)],
        (recv1, conv, cols, rows, at_mat, a_mat, hid, cot, sig),
        flops=8 << 30,
    )
    send3, back, hop, ext, ext_hub, sig_u = stepped(
        rows_kernel,
        [((NODE, EXT), BF), (field, BF), (field, BF), ((T1, EXT, C), BF), (edge, BF),
         (edge4, BF)],
        (me, hub_owner, recv2, cols, rows, conv, hub_sig, hub_sig, a_hub, hop_part, back_part,
         at_mat),
        ("all", "all", "all", "all", "this", "next", "all", "this", "this", "all"),
        ("lanes", "this", "this", "this", "this", "all"),
        smem=2,
        scratch=[pltpu.VMEM((NODE, NODE), BF), pltpu.VMEM((NODE, EXT - NODE), BF)],
        flops=4 << 30,
    )
    recv3 = swap(send3.reshape(DOM, 8, EXT), "dom").reshape(NODE, EXT)
    keep, give = stepped(
        weight_kernel,
        [(half, F32), (half, F32)],
        (core, conv, mix, hop, cot, back, ext, sig, sig, sig_h, sig_h, sig_u, sig_u, fac_f, fac_g,
         mix0),
        ("all", "all", "this", "this", "this", "this", "this", "next", "this", "next", "this",
         "next", "this", "this", "all"),
        ("all", "all"),
        smem=1,
        scratch=[pltpu.VMEM((6, C, C), F32)],
        flops=8 << 30,
    )
    pairs = [(i, i ^ 1) for i in range(DOM)]
    rounds = [[(i, (i + k) % BATCH) for i in range(BATCH)] for k in range(BATCH)]
    got = lax.ppermute(give, "dom", pairs)
    parts = call(
        pair_kernel, [(chunk, BF)] * BATCH, (batch, keep, got), 8, smem=1, flops=1 << 26
    )
    parts = [parts[0]] + [
        lax.ppermute(parts[k], "batch", rounds[k]) for k in range(1, BATCH)
    ]
    (send4,) = call(
        second_hub_kernel,
        [((DOM, 8, C + BLK), BF)],
        (me, hub_owner, recv3, *parts),
        8,
        smem=2,
        flops=1 << 28,
    )
    recv4 = swap(send4, "dom")
    mixed, two, gh, hop_hub = call(
        near_kernel,
        [(field, F32), (field, F32), (field, F32), (edge, BF)],
        (recv3, cols, rows, a_mat, mix, hop, hid, sig, ext_hub, ext, back, cot),
        flops=8 << 30,
    )
    recv4, mixed, two, gh, hop_hub = lax.optimization_barrier((recv4, mixed, two, gh, hop_hub))
    (send5,) = call(spread_kernel, [((DOM, 8, BLK), BF)], (recv4,), 6, flops=1 << 26)
    recv5 = swap(send5, "dom").reshape(chunk)
    recv4 = recv4.reshape(NODE, C + BLK)
    (sgrad,) = call(
        signal_kernel,
        [((HIST, NODE, C), BF)],
        (me, hub_owner, recv4, rows, mix, conv, gh, fac_f, fac_g, cot),
        smem=2,
        flops=8 << 30,
    )
    sgrad = jnp.transpose(sgrad, (1, 0, 2))
    vmem, keep_place = (pl.BlockSpec(memory_space=m) for m in (pltpu.VMEM, pl.ANY))
    recv5, sgrad = pl.pallas_call(
        tie_kernel,
        out_shape=[jax.ShapeDtypeStruct(x.shape, x.dtype) for x in (recv5, sgrad)],
        in_specs=[vmem, keep_place],
        out_specs=[vmem, keep_place],
        input_output_aliases={1: 1},
        compiler_params=pltpu.CompilerParams(vmem_limit_bytes=4 << 20),
    )(recv5, sgrad)
    mine = [recv5] + [lax.ppermute(recv5, "batch", rounds[k]) for k in range(1, BATCH)]
    (layer,) = call(
        layer_kernel,
        [(field, BF)],
        (recv4, cols, a_hub, mix, hop_hub, mixed, two),
        flops=4 << 30,
    )
    mine, layer = lax.optimization_barrier((mine, layer))
    other = [lax.ppermute(one, "dom", pairs) for one in mine]
    conv_grad, mix_grad = call(
        scale_kernel,
        [((4, C, C), F32), ((3, C, C), F32)],
        (core, batch, *mine, *other),
        10,
        smem=2,
        flops=1 << 20,
    )
    layer = jnp.transpose(layer, (1, 0, 2))[:, None]
    return layer, sgrad[:, None], conv_grad.reshape(2, 2, C, C), mix_grad


def solution(mesh):
    placed = (
        P("dom", "batch", None, None),
        P("dom", "batch", None, None),
        P(),
        P(),
        P("dom", None),
        P("dom", None),
        P("dom", None, None),
        P("dom"),
        P("dom"),
        P("dom"),
        P(),
        P(),
    )
    return jax.shard_map(
        body,
        mesh=mesh,
        in_specs=placed,
        out_specs=(P("dom", "batch", None, None), P("dom", "batch", None, None), P(), P()),
        check_vma=False,
    )
```

```python
import math

import jax
import jax.numpy as jnp
from jax import lax
from jax.experimental import pallas as pl
from jax.experimental.pallas import tpu as pltpu
from jax.sharding import PartitionSpec as P

BF = jnp.bfloat16
F32 = jnp.float32
I32 = jnp.int32
NODE = 512
EXT = 768
BLK = 128
C = 256
T1 = 3
HIST = 4
DOM = 64
BATCH = 4
OWNERS = 8
HUB_PER = 16
TILES = 16
PIECES = 7
CHUNK = 448


def nn(a, b):
    return jnp.dot(a, b, preferred_element_type=F32)


def nt(a, b):
    return lax.dot_general(a, b, (((1,), (1,)), ((), ())), preferred_element_type=F32)


def tn(a, b):
    return lax.dot_general(a, b, (((0,), (0,)), ((), ())), preferred_element_type=F32)


def iota(shape, dim):
    return lax.broadcasted_iota(I32, shape, dim)


def hot(mask):
    return jnp.where(mask, 1.0, 0.0).astype(BF)


def pick_rows(column, count):
    return hot(column == iota((column.shape[0], count), 1))


def put_rows(row, count):
    return hot(row == iota((count, row.shape[1]), 0))


def gates(early, late, conv):
    filt = nn(early, conv[0, 0]) + nn(late, conv[0, 1])
    gate = nn(early, conv[1, 0]) + nn(late, conv[1, 1])
    th = jnp.tanh(filt)
    sg = jax.nn.sigmoid(gate)
    return (th * sg).astype(BF), sg * (1.0 - th * th), th * sg * (1.0 - sg)


def call(kernel, outs, args, mib=60, smem=0, scratch=(), flops=0):
    vmem = pl.BlockSpec(memory_space=pltpu.VMEM)
    return pl.pallas_call(
        kernel,
        out_shape=[jax.ShapeDtypeStruct(s, d) for s, d in outs],
        in_specs=[pl.BlockSpec(memory_space=pltpu.SMEM)] * smem + [vmem] * (len(args) - smem),
        out_specs=[vmem] * len(outs),
        scratch_shapes=list(scratch),
        compiler_params=pltpu.CompilerParams(vmem_limit_bytes=mib << 20),
        cost_estimate=pl.CostEstimate(flops=flops, bytes_accessed=8 << 20, transcendentals=0),
    )(*args)


def stepped(kernel, outs, args, kinds, out_kinds, smem=0, scratch=(), flops=0):
    def spec(shape, kind):
        if kind == "all":
            return pl.BlockSpec(shape, lambda t: (0,) * len(shape))
        if kind == "lanes":
            return pl.BlockSpec((shape[0], C), lambda t: (0, t))
        ahead = 1 if kind == "next" else 0
        return pl.BlockSpec((1,) + shape[1:], lambda t: (t + ahead,) + (0,) * (len(shape) - 1))

    return pl.pallas_call(
        kernel,
        grid=(T1,),
        out_shape=[jax.ShapeDtypeStruct(s, d) for s, d in outs],
        in_specs=[pl.BlockSpec(memory_space=pltpu.SMEM)] * smem
        + [spec(x.shape, k) for x, k in zip(args[smem:], kinds)],
        out_specs=[spec(s, k) for (s, d), k in zip(outs, out_kinds)],
        scratch_shapes=list(scratch),
        compiler_params=pltpu.CompilerParams(vmem_limit_bytes=60 << 20),
        cost_estimate=pl.CostEstimate(flops=flops, bytes_accessed=8 << 20, transcendentals=0),
    )(*args)


def high_low(x):
    return (x >> 4).astype(F32).astype(BF), (x & 15).astype(F32).astype(BF)


def add_tiles(acc, trow, tcol, tmask, tiles, low):
    acc[...] = jnp.zeros_like(acc)

    def add(i, carry):
        @pl.when((tmask[i] == 1) & (tcol[i] >= low))
        def _():
            acc[(tcol[i] - low) * 4 + trow[i]] += tiles[i].astype(F32)

        return carry

    lax.fori_loop(0, TILES, add, 0)


def slot_of(me, owners):
    slot = jnp.int32(-1)
    for o in range(OWNERS):
        slot = jnp.where(owners[o] == me[0], o, slot)
    return slot


def own_hub_block(me, owners, rows, recv):
    at = pl.multiple_of(jnp.maximum(slot_of(me, owners), 0) * DOM, DOM)
    return recv[pl.ds(at, DOM), 0:C], rows[3:4, 0:DOM]


def put_step(target, t):
    at = iota((NODE, DOM), 1)
    return hot((target == iota((NODE, DOM), 0)) & ((at & 3) == t))


def start_kernel(
    trow, tcol, tmask, me, owners, tiles, used_rows, used_mask, hubs, cot, sig,
    cols_out, rows_out, send, acc, far,
):
    slot = slot_of(me, owners)
    used = jnp.where(used_mask[...] == 1, used_rows[...] + 1, 0)
    held = jnp.where(iota((OWNERS, HUB_PER), 0) == slot, hubs[...] + 1, 0)
    held = jnp.broadcast_to(jnp.sum(held, 0, keepdims=True), (8, HUB_PER))
    held_high, held_low = high_low(held)
    j16 = iota((HUB_PER, DOM), 0)
    q16 = iota((HUB_PER, DOM), 1)
    line = iota((8, DOM), 0)
    values = jnp.where(line == 0, used[0:1], jnp.where(line == 1, used[1:2], 0))
    for i in range(2):
        lay = hot((j16 == 2 * (q16 & 7) + i) & ((q16 >> 3) == slot))
        wide = (16.0 * nn(held_high, lay) + nn(held_low, lay)).astype(I32)
        values = jnp.where(line == 2 + i, wide, values)
    high, low = high_low(values)

    def down(count, shift):
        pick = hot((iota((count, DOM), 0) >> shift) == iota((count, DOM), 1))
        return (16.0 * nt(pick, high) + nt(pick, low)).astype(I32) - 1

    def along(count, shift):
        pick = hot((iota((DOM, count), 1) >> shift) == iota((DOM, count), 0))
        return (16.0 * nn(high, pick) + nn(low, pick)).astype(I32) - 1

    by_row = down(NODE, 3)
    m = iota((NODE, 1), 0)
    j = m & 7
    first, second, hub0, hub1 = [by_row[:, k : k + 1] for k in range(4)]
    pick_sig = jnp.where(j == 0, first, jnp.where(j == 1, second, -1))
    pick_sig = jnp.where(j == 2, hub0, jnp.where(j == 3, hub1, pick_sig))
    two = 2 * (m >> 3) + (j & 1)
    not_mine = (m >> 6) != slot
    pick_ext = jnp.where((j >> 1) == 2, two, -1)
    pick_ext = jnp.where(((j >> 1) == 1) & not_mine, BLK + two, pick_ext)
    last = [
        jnp.where(j == 6, first, jnp.where(j == 7, hub1, -1)),
        jnp.where(j == 6, second, -1),
        jnp.where(j == 6, hub0, -1),
    ]
    by_hub = down(BLK, 1)
    odd = (iota((BLK, 1), 0) & 1) == 1
    hub_col = jnp.where(odd, by_hub[:, 3:4], by_hub[:, 2:3])
    lane = iota((NODE, BLK), 1)
    hub_wide = jnp.concatenate([hub_col, jnp.full((NODE - BLK, 1), -1, I32)], 0)
    cols_out[...] = jnp.where(
        lane == 0, pick_sig, jnp.where(lane == 1, pick_ext, jnp.where(lane == 2, hub_wide, -1))
    )
    flat = along(NODE, 3)
    mr = iota((1, NODE), 1)
    jr = mr & 7
    back_row = jnp.where(jr == 4, flat[0:1], jnp.where(jr == 5, flat[1:2], -1))
    flat_hub = along(BLK, 1)
    odd = (iota((1, BLK), 1) & 1) == 1
    hub_row = jnp.where(odd, flat_hub[3:4], flat_hub[2:3])
    hub_row = jnp.concatenate([hub_row, jnp.full((1, NODE - BLK), -1, I32)], 1)
    j16 = iota((HUB_PER, NODE), 0)
    at = iota((HUB_PER, NODE), 1)
    lay = hot((j16 == 2 * (at >> 3) + ((at >> 2) & 1)) & (at < DOM))
    hub_mine = (16.0 * nn(held_high, lay) + nn(held_low, lay)).astype(I32)[0:1] - 1
    line = iota((8, NODE), 0)
    rows_out[...] = jnp.where(
        line == 0, back_row, jnp.where(line == 2, hub_row, jnp.where(line == 3, hub_mine, -1))
    )

    add_tiles(acc, trow, tcol, tmask, tiles, 4)
    for r in range(4):
        for c in range(2):
            block = acc[c * 4 + r]
            far[c * BLK : (c + 1) * BLK, r * BLK : (r + 1) * BLK] = block.T.astype(BF)
    from_sig = pick_rows(pick_sig, NODE)
    from_ext = pick_rows(pick_ext, EXT - NODE)
    for t in range(T1):
        ext = nn(far[...], cot[t]).astype(BF)
        out = (
            nn(from_ext, ext)
            + nn(from_sig, sig[t])
            + nn(pick_rows(last[t], NODE), sig[HIST - 1])
        )
        send[:, t * C : (t + 1) * C] = out.astype(BF)


def own_kernel(
    trow, tcol, tmask, tiles, conv, sig, cot, a_out, a_hub, at_out, hid, fac_f, fac_g, mix0, acc
):
    add_tiles(acc, trow, tcol, tmask, tiles, 0)
    for r in range(4):
        for c in range(6):
            block = acc[c * 4 + r]
            a_out[r * BLK : (r + 1) * BLK, c * BLK : (c + 1) * BLK] = block.astype(BF)
            at_out[c * BLK : (c + 1) * BLK, r * BLK : (r + 1) * BLK] = block.T.astype(BF)
    a_hub[...] = a_out[:, NODE + BLK :]
    total = jnp.zeros((C, C), F32)
    weights = conv
    for t in range(T1):
        h, p, q = gates(sig[t], sig[t + 1], weights)
        hid[t] = h
        fac_f[t] = p
        fac_g[t] = q
        total += tn(h, cot[t])
    mix0[...] = total


def hub_blocks(recv, owner, with_last):
    row = iota((8, NODE), 0)
    m = iota((8, NODE), 1)
    which = row >> 2
    step = row & 3
    forward = jnp.zeros((8, C), F32)
    backward = jnp.zeros((8, C), F32)
    for c in range(T1):
        block = recv[:, c * C : (c + 1) * C]
        f = (step == c) & (m == owner * 8 + 2 + which)
        if with_last and c == 2:
            f = f | ((row == 3) & (m == owner * 8 + 6))
        if with_last and c == 0:
            f = f | ((row == 7) & (m == owner * 8 + 7))
        b = (step == c) & ((m & 7) == 2 + which) & ((m >> 3) != owner)
        forward += nn(hot(f), block)
        backward += nn(hot(b), block)
    return forward, backward


def hub_kernel(me, owners, recv, send):
    owner = owners[me[0] >> 3]
    forward, backward = hub_blocks(recv, owner, True)
    at_owner = iota((DOM, 8, C), 0) == owner
    send[...] = jnp.where(at_owner, backward[None], forward[None]).astype(BF)


def halo_kernel(
    recv, conv, cols, rows, at_mat, a_mat, hid, cot, sig, back, hop, sig_x, hub_sig
):
    r = iota((BLK, NODE), 0)
    m = iota((BLK, NODE), 1)
    base = (r >> 1) * 8
    odd = r & 1
    pick0 = hot(m == base + odd)
    pick3a = hot((odd == 0) & (m == base + 6))
    pick3b = hot((odd == 1) & (m == base + 6))
    blocks = [recv[:, t * C : (t + 1) * C] for t in range(T1)]
    weights = conv
    far = [nn(pick0, block).astype(BF) for block in blocks]
    far.append((nn(pick3a, blocks[0]) + nn(pick3b, blocks[1])).astype(BF))
    for t in range(HIST):
        sig_x[t] = far[t]
    hid_x = [gates(far[t], far[t + 1], weights)[0] for t in range(T1)]
    put_halo = put_rows(rows[0:1, :], NODE)
    put_hub_own = put_rows(rows[2:3, 0:BLK], NODE)
    for t in range(T1):
        hub = nn(at_mat[NODE + BLK :, :], cot[t]).astype(BF)
        back[t] = (
            nn(at_mat[:NODE, :], cot[t]) + nn(put_halo, blocks[t]) + nn(put_hub_own, hub)
        )
        hop[t] = nn(a_mat[:, :NODE], hid[t]) + nn(a_mat[:, NODE : NODE + BLK], hid_x[t])
    own_pick = pick_rows(cols[0:BLK, 2:3], NODE)
    for t in range(HIST):
        hub_sig[t] = nn(own_pick, sig[t]).astype(BF)


def rows_kernel(
    me, owners, recv, cols, rows, conv, hub0, hub1, a_hub, hop_part, back_part, at_mat,
    send, back_out, hop_out, ext_out, ext_hub, sig_x, pick_sig, pick_ext,
):
    t = pl.program_id(0)

    @pl.when(t == 0)
    def _():
        pick_sig[...] = pick_rows(cols[:, 0:1], NODE)
        pick_ext[...] = pick_rows(cols[:, 1:2], EXT - NODE)

    r = iota((BLK, NODE), 0)
    m = iota((BLK, NODE), 1)
    base = (r >> 1) * 8 + (r & 1) * 4
    own_node = cols[0:BLK, 2:3]
    hubs = recv[...]
    far = []
    for s, hub_sig in ((0, hub0), (1, hub1)):
        hub_pick = hot((m == base + (t + s)) & (own_node < 0))
        far.append((nn(hub_pick, hubs) + hub_sig[0].astype(F32)).astype(BF))
        sig_x[t + s] = far[s]
    mine, target = own_hub_block(me, owners, rows, recv)
    h = gates(far[0], far[1], conv)[0]
    hop = (hop_part[0] + nn(a_hub[...], h)).astype(BF)
    hop_out[0] = hop
    back = (back_part[0] + nn(put_step(target, t), mine)).astype(BF)
    back_out[0] = back
    ext = nn(at_mat[...], back).astype(BF)
    out = nn(pick_sig[...], hop) + nn(pick_ext[...], ext[NODE:])
    send[...] = out.astype(BF)
    ext_out[0] = ext
    ext_hub[0] = ext[NODE + BLK :]


def weight_kernel(
    core, conv, mix, hop, cot, back, ext, sig0, sig1, halo0, halo1, hub0, hub1, fac_f, fac_g,
    mix0, keep, give, acc,
):
    t = pl.program_id(0)

    @pl.when(t == 0)
    def _():
        acc[...] = jnp.zeros_like(acc)

    acc[4] += tn(hop[0], cot[0])
    acc[5] += tn(hop[0], back[0])
    through = nt(ext[0], mix[2])
    gh = nt(cot[0], mix[0]) + nt(back[0], mix[1]) + through[:NODE]
    far_sig = (
        jnp.concatenate([halo0[0], hub0[0]], 0),
        jnp.concatenate([halo1[0], hub1[0]], 0),
    )
    _, p, q = gates(far_sig[0], far_sig[1], conv)
    own = ((gh * fac_f[0]).astype(BF), (gh * fac_g[0]).astype(BF))
    far = ((through[NODE:] * p).astype(BF), (through[NODE:] * q).astype(BF))
    for s, sig in ((0, sig0), (1, sig1)):
        for k in range(2):
            acc[2 * k + s] += tn(sig[0], own[k]) + tn(far_sig[s], far[k])

    @pl.when(t == T1 - 1)
    def _():
        first = core[0] == 0
        mats = (acc[0], acc[1], acc[2], acc[3], mix0[...], acc[4], acc[5])
        pieces = [x[:, s * BLK : (s + 1) * BLK] for x in mats for s in range(2)]
        for j in range(PIECES):
            low, high = pieces[j], pieces[PIECES + j]
            give[j * C : (j + 1) * C, :] = jnp.where(first, high, low)
            keep[j * C : (j + 1) * C, :] = jnp.where(first, low, high)


def pair_kernel(batch, keep, got, *outs):
    mine, other = keep, got
    for k in range(BATCH):
        at = pl.ds(pl.multiple_of(((batch[0] + k) & (BATCH - 1)) * CHUNK, DOM), CHUNK)
        outs[k][...] = (mine[at, :] + other[at, :]).astype(BF)


def same_slot(n, m):
    return (n == (m >> 3) * PIECES + (m & 7)) & ((m & 7) < PIECES)


def second_hub_kernel(me, owners, recv, part0, part1, part2, part3, send):
    owner = owners[me[0] >> 3]
    forward, backward = hub_blocks(recv, owner, False)
    total = part0[...].astype(F32) + part1[...].astype(F32)
    total += part2[...].astype(F32) + part3[...].astype(F32)
    at_owner = iota((DOM, 8, C), 0) == owner
    send[:, :, 0:C] = jnp.where(at_owner, backward[None], forward[None]).astype(BF)
    place = hot(same_slot(iota((NODE, CHUNK), 1), iota((NODE, CHUNK), 0)))
    send[:, :, C:] = nn(place, total.astype(BF)).astype(BF).reshape(DOM, 8, BLK)


def spread_kernel(recv, send):
    even = jnp.zeros((8, BLK), F32)
    odd = jnp.zeros((8, BLK), F32)
    for p in range(0, DOM, 2):
        even += recv[p, :, C:].astype(F32)
        odd += recv[p + 1, :, C:].astype(F32)
    is_odd = (iota((DOM, 8, BLK), 0) & 1) == 1
    send[...] = jnp.where(is_odd, odd[None], even[None]).astype(BF)


def near_kernel(
    recv, cols, rows, a_mat, mix, hop_ref, hid, sig, ext_hub, ext, back_ref, cot,
    mixed, two, gh_out, hop_hub,
):
    r = iota((BLK, NODE), 0)
    m = iota((BLK, NODE), 1)
    pick0 = hot(m == (r >> 1) * 8 + (r & 1))
    own_pick = pick_rows(cols[0:BLK, 2:3], NODE)
    put_halo = put_rows(rows[0:1, :], NODE)
    put_hub_own = put_rows(rows[2:3, 0:BLK], NODE)
    for t in range(T1):
        block = recv[:, t * C : (t + 1) * C]
        hop = hop_ref[t]
        rows_halo = nn(pick0, block).astype(BF)
        two[t] = nn(a_mat[:, :NODE], hop) + nn(a_mat[:, NODE : NODE + BLK], rows_halo)
        hop_hub[t] = nn(own_pick, hop).astype(BF)
        mixed[t] = sig[t + 1].astype(F32) + nn(hid[t], mix[0]) + nn(hop, mix[1])
        back = (nn(put_halo, block) + nn(put_hub_own, ext_hub[t])).astype(BF)
        own = nt(cot[t], mix[0]) + nt(back_ref[t], mix[1]) + nt(ext[t, 0:NODE, :], mix[2])
        gh_out[t] = own + nt(back, mix[2])


def signal_kernel(
    me, owners, recv, rows, mix, conv, gh_ref, fac_f, fac_g, cot, sgrad
):
    mine, target = own_hub_block(me, owners, rows, recv)
    for t in range(T1):
        back = nn(put_step(target, t), mine).astype(BF)
        gh = gh_ref[t] + nt(back, mix[2])
        gf = (gh * fac_f[t]).astype(BF)
        gg = (gh * fac_g[t]).astype(BF)
        early = nt(gf, conv[0, 0]) + nt(gg, conv[1, 0])
        late = nt(gf, conv[0, 1]) + nt(gg, conv[1, 1]) + cot[t].astype(F32)
        if t == 0:
            sgrad[0] = early.astype(BF)
        else:
            sgrad[t] = (early + carried).astype(BF)
        carried = late
    sgrad[T1] = carried.astype(BF)


def layer_kernel(recv, cols, a_hub, mix, hop_hub, mixed, two_ref, layer):
    r = iota((BLK, NODE), 0)
    m = iota((BLK, NODE), 1)
    base = (r >> 1) * 8 + (r & 1) * 4
    own_node = cols[0:BLK, 2:3]
    hubs = recv[:, 0:C]
    for t in range(T1):
        hub_pick = hot((m == base + t) & (own_node < 0))
        rows_hub = (nn(hub_pick, hubs) + hop_hub[t].astype(F32)).astype(BF)
        two = (two_ref[t] + nn(a_hub[...], rows_hub)).astype(BF)
        layer[t] = (mixed[t] + nn(two, mix[2])).astype(BF)


def tie_kernel(chunk, kept, chunk_out, kept_out):
    del kept, kept_out
    pack = hot(same_slot(iota((CHUNK, NODE), 0), iota((CHUNK, NODE), 1)))
    chunk_out[...] = nn(pack, chunk[...]).astype(BF)


def scale_kernel(core, batch, *refs):
    mine, other = refs[0:BATCH], refs[BATCH : 2 * BATCH]
    conv_grad, mix_grad, held = refs[2 * BATCH :]
    factor = 1.0 / math.sqrt(NODE * DOM * BATCH * T1)
    first = core[0] == 0
    for k in range(BATCH):
        block = (batch[0] + BATCH - k) & (BATCH - 1)
        at = pl.ds(pl.multiple_of(block * CHUNK, DOM), CHUNK)
        held[0, at, :] = jnp.where(first, mine[k][...], other[k][...])
        held[1, at, :] = jnp.where(first, other[k][...], mine[k][...])
    for p in range(2 * PIECES):
        j = p % PIECES
        piece = held[p // PIECES, j * C : (j + 1) * C, :].astype(F32) * factor
        lanes = slice((p % 2) * BLK, (p % 2 + 1) * BLK)
        if p < 8:
            conv_grad[p // 2, :, lanes] = piece
        else:
            mix_grad[p // 2 - 4, :, lanes] = piece


def swap(x, axis):
    return lax.all_to_all(x, axis, split_axis=0, concat_axis=0, tiled=True)


def body(
    signal,
    cotangent,
    conv,
    mix,
    send_rows,
    send_mask,
    tile_vals,
    tile_row,
    tile_col,
    tile_mask,
    hub_owner,
    hub_rows,
):
    me = lax.axis_index("dom").astype(I32)
    core = (me & 1).reshape(1)
    me = me.reshape(1)
    batch = lax.axis_index("batch").astype(I32).reshape(1)
    sig = jnp.transpose(signal[:, 0], (1, 0, 2))
    cot = jnp.transpose(cotangent[:, 0], (1, 0, 2))

    field = (T1, NODE, C)
    edge = (T1, BLK, C)
    edge4 = (HIST, BLK, C)
    half = (PIECES * C, BLK)
    chunk = (CHUNK, BLK)
    cols, rows, send1 = call(
        start_kernel,
        [((NODE, BLK), I32), ((8, NODE), I32), ((NODE, EXT), BF)],
        (tile_row, tile_col, tile_mask, me, hub_owner, tile_vals, send_rows.T, send_mask.T,
         hub_rows, cot, sig),
        smem=5,
        scratch=[pltpu.VMEM((8, BLK, BLK), F32), pltpu.VMEM((EXT - NODE, NODE), BF)],
        flops=2 << 30,
    )
    recv1 = swap(send1.reshape(DOM, 8, EXT), "dom").reshape(NODE, EXT)
    a_mat, a_hub, at_mat, hid, fac_f, fac_g, mix0 = call(
        own_kernel,
        [((NODE, EXT), BF), ((NODE, BLK), BF), ((EXT, NODE), BF), (field, BF), (field, F32),
         (field, F32), ((C, C), F32)],
        (tile_row, tile_col, tile_mask, tile_vals, conv, sig, cot),
        smem=3,
        scratch=[pltpu.VMEM((24, BLK, BLK), F32)],
        flops=8 << 30,
    )
    (send2,) = call(
        hub_kernel, [((DOM, 8, C), BF)], (me, hub_owner, recv1), 8, smem=2, flops=1 << 28
    )
    recv2 = swap(send2, "dom").reshape(NODE, C)
    back_part, hop_part, sig_h, hub_sig = call(
        halo_kernel,
        [(field, F32), (field, F32), (edge4, BF), (edge4, BF)],
        (recv1, conv, cols, rows, at_mat, a_mat, hid, cot, sig),
        flops=8 << 30,
    )
    send3, back, hop, ext, ext_hub, sig_u = stepped(
        rows_kernel,
        [((NODE, EXT), BF), (field, BF), (field, BF), ((T1, EXT, C), BF), (edge, BF),
         (edge4, BF)],
        (me, hub_owner, recv2, cols, rows, conv, hub_sig, hub_sig, a_hub, hop_part, back_part,
         at_mat),
        ("all", "all", "all", "all", "this", "next", "all", "this", "this", "all"),
        ("lanes", "this", "this", "this", "this", "all"),
        smem=2,
        scratch=[pltpu.VMEM((NODE, NODE), BF), pltpu.VMEM((NODE, EXT - NODE), BF)],
        flops=4 << 30,
    )
    recv3 = swap(send3.reshape(DOM, 8, EXT), "dom").reshape(NODE, EXT)
    keep, give = stepped(
        weight_kernel,
        [(half, F32), (half, F32)],
        (core, conv, mix, hop, cot, back, ext, sig, sig, sig_h, sig_h, sig_u, sig_u, fac_f, fac_g,
         mix0),
        ("all", "all", "this", "this", "this", "this", "this", "next", "this", "next", "this",
         "next", "this", "this", "all"),
        ("all", "all"),
        smem=1,
        scratch=[pltpu.VMEM((6, C, C), F32)],
        flops=8 << 30,
    )
    pairs = [(i, i ^ 1) for i in range(DOM)]
    rounds = [[(i, (i + k) % BATCH) for i in range(BATCH)] for k in range(BATCH)]
    got = lax.ppermute(give, "dom", pairs)
    parts = call(
        pair_kernel, [(chunk, BF)] * BATCH, (batch, keep, got), 8, smem=1, flops=1 << 26
    )
    parts = [parts[0]] + [
        lax.ppermute(parts[k], "batch", rounds[k]) for k in range(1, BATCH)
    ]
    (send4,) = call(
        second_hub_kernel,
        [((DOM, 8, C + BLK), BF)],
        (me, hub_owner, recv3, *parts),
        8,
        smem=2,
        flops=1 << 28,
    )
    recv4 = swap(send4, "dom")
    mixed, two, gh, hop_hub = call(
        near_kernel,
        [(field, F32), (field, F32), (field, F32), (edge, BF)],
        (recv3, cols, rows, a_mat, mix, hop, hid, sig, ext_hub, ext, back, cot),
        flops=8 << 30,
    )
    recv4, mixed, two, gh, hop_hub = lax.optimization_barrier((recv4, mixed, two, gh, hop_hub))
    (send5,) = call(spread_kernel, [((DOM, 8, BLK), BF)], (recv4,), 6, flops=1 << 26)
    recv5 = swap(send5, "dom").reshape(NODE, BLK)
    recv4 = recv4.reshape(NODE, C + BLK)
    (sgrad,) = call(
        signal_kernel,
        [((HIST, NODE, C), BF)],
        (me, hub_owner, recv4, rows, mix, conv, gh, fac_f, fac_g, cot),
        smem=2,
        flops=8 << 30,
    )
    sgrad = jnp.transpose(sgrad, (1, 0, 2))
    vmem, keep_place = (pl.BlockSpec(memory_space=m) for m in (pltpu.VMEM, pl.ANY))
    recv5, sgrad = pl.pallas_call(
        tie_kernel,
        out_shape=[jax.ShapeDtypeStruct(x, BF) for x in (chunk, sgrad.shape)],
        in_specs=[vmem, keep_place],
        out_specs=[vmem, keep_place],
        input_output_aliases={1: 1},
        compiler_params=pltpu.CompilerParams(vmem_limit_bytes=4 << 20),
    )(recv5, sgrad)
    mine = [recv5] + [lax.ppermute(recv5, "batch", rounds[k]) for k in range(1, BATCH)]
    (layer,) = call(
        layer_kernel,
        [(field, BF)],
        (recv4, cols, a_hub, mix, hop_hub, mixed, two),
        flops=4 << 30,
    )
    mine, layer = lax.optimization_barrier((mine, layer))
    other = [lax.ppermute(one, "dom", pairs) for one in mine]
    conv_grad, mix_grad = call(
        scale_kernel,
        [((4, C, C), F32), ((3, C, C), F32)],
        (core, batch, *mine, *other),
        10,
        smem=2,
        scratch=[pltpu.VMEM((2, PIECES * C, BLK), BF)],
        flops=1 << 20,
    )
    layer = jnp.transpose(layer, (1, 0, 2))[:, None]
    return layer, sgrad[:, None], conv_grad.reshape(2, 2, C, C), mix_grad


def solution(mesh):
    placed = (
        P("dom", "batch", None, None),
        P("dom", "batch", None, None),
        P(),
        P(),
        P("dom", None),
        P("dom", None),
        P("dom", None, None),
        P("dom"),
        P("dom"),
        P("dom"),
        P(),
        P(),
    )
    return jax.shard_map(
        body,
        mesh=mesh,
        in_specs=placed,
        out_specs=(P("dom", "batch", None, None), P("dom", "batch", None, None), P(), P()),
        check_vma=False,
    )
```

```python
import math

import jax
import jax.numpy as jnp
from jax import lax
from jax.experimental import pallas as pl
from jax.experimental.pallas import tpu as pltpu
from jax.sharding import PartitionSpec as P

BF = jnp.bfloat16
F32 = jnp.float32
I32 = jnp.int32
NODE = 512
EXT = 768
BLK = 128
C = 256
T1 = 3
HIST = 4
DOM = 64
BATCH = 4
OWNERS = 8
HUB_PER = 16
TILES = 16
PIECES = 7
CHUNK = 448


def nn(a, b):
    return jnp.dot(a, b, preferred_element_type=F32)


def nt(a, b):
    return lax.dot_general(a, b, (((1,), (1,)), ((), ())), preferred_element_type=F32)


def tn(a, b):
    return lax.dot_general(a, b, (((0,), (0,)), ((), ())), preferred_element_type=F32)


def iota(shape, dim):
    return lax.broadcasted_iota(I32, shape, dim)


def hot(mask):
    return jnp.where(mask, 1.0, 0.0).astype(BF)


def pick_rows(column, count):
    return hot(column == iota((column.shape[0], count), 1))


def put_rows(row, count):
    return hot(row == iota((count, row.shape[1]), 0))


def gates(early, late, conv):
    filt = nn(early, conv[0, 0]) + nn(late, conv[0, 1])
    gate = nn(early, conv[1, 0]) + nn(late, conv[1, 1])
    th = jnp.tanh(filt)
    sg = jax.nn.sigmoid(gate)
    return (th * sg).astype(BF), sg * (1.0 - th * th), th * sg * (1.0 - sg)


def call(kernel, outs, args, mib=60, smem=0, scratch=(), flops=0):
    vmem = pl.BlockSpec(memory_space=pltpu.VMEM)
    return pl.pallas_call(
        kernel,
        out_shape=[jax.ShapeDtypeStruct(s, d) for s, d in outs],
        in_specs=[pl.BlockSpec(memory_space=pltpu.SMEM)] * smem + [vmem] * (len(args) - smem),
        out_specs=[vmem] * len(outs),
        scratch_shapes=list(scratch),
        compiler_params=pltpu.CompilerParams(vmem_limit_bytes=mib << 20),
        cost_estimate=pl.CostEstimate(flops=flops, bytes_accessed=8 << 20, transcendentals=0),
    )(*args)


def stepped(kernel, outs, args, kinds, out_kinds, smem=0, scratch=(), flops=0):
    def spec(shape, kind):
        if kind == "all":
            return pl.BlockSpec(shape, lambda t: (0,) * len(shape))
        if kind == "lanes":
            return pl.BlockSpec((shape[0], C), lambda t: (0, t))
        ahead = 1 if kind == "next" else 0
        return pl.BlockSpec((1,) + shape[1:], lambda t: (t + ahead,) + (0,) * (len(shape) - 1))

    return pl.pallas_call(
        kernel,
        grid=(T1,),
        out_shape=[jax.ShapeDtypeStruct(s, d) for s, d in outs],
        in_specs=[pl.BlockSpec(memory_space=pltpu.SMEM)] * smem
        + [spec(x.shape, k) for x, k in zip(args[smem:], kinds)],
        out_specs=[spec(s, k) for (s, d), k in zip(outs, out_kinds)],
        scratch_shapes=list(scratch),
        compiler_params=pltpu.CompilerParams(vmem_limit_bytes=60 << 20),
        cost_estimate=pl.CostEstimate(flops=flops, bytes_accessed=8 << 20, transcendentals=0),
    )(*args)


def high_low(x):
    return (x >> 4).astype(F32).astype(BF), (x & 15).astype(F32).astype(BF)


def add_tiles(acc, trow, tcol, tmask, tiles, low):
    acc[...] = jnp.zeros_like(acc)

    def add(i, carry):
        @pl.when((tmask[i] == 1) & (tcol[i] >= low))
        def _():
            acc[(tcol[i] - low) * 4 + trow[i]] += tiles[i].astype(F32)

        return carry

    lax.fori_loop(0, TILES, add, 0)


def slot_of(me, owners):
    slot = jnp.int32(-1)
    for o in range(OWNERS):
        slot = jnp.where(owners[o] == me[0], o, slot)
    return slot


def own_hub_block(me, owners, rows, recv):
    at = pl.multiple_of(jnp.maximum(slot_of(me, owners), 0) * DOM, DOM)
    return recv[pl.ds(at, DOM), 0:C], rows[3:4, 0:DOM]


def put_step(target, t):
    at = iota((NODE, DOM), 1)
    return hot((target == iota((NODE, DOM), 0)) & ((at & 3) == t))


def start_kernel(
    trow, tcol, tmask, me, owners, tiles, used_rows, used_mask, hubs, cot, sig,
    cols_out, rows_out, send, acc, far,
):
    slot = slot_of(me, owners)
    used = jnp.where(used_mask[...] == 1, used_rows[...] + 1, 0)
    held = jnp.where(iota((OWNERS, HUB_PER), 0) == slot, hubs[...] + 1, 0)
    held = jnp.broadcast_to(jnp.sum(held, 0, keepdims=True), (8, HUB_PER))
    held_high, held_low = high_low(held)
    j16 = iota((HUB_PER, DOM), 0)
    q16 = iota((HUB_PER, DOM), 1)
    line = iota((8, DOM), 0)
    values = jnp.where(line == 0, used[0:1], jnp.where(line == 1, used[1:2], 0))
    for i in range(2):
        lay = hot((j16 == 2 * (q16 & 7) + i) & ((q16 >> 3) == slot))
        wide = (16.0 * nn(held_high, lay) + nn(held_low, lay)).astype(I32)
        values = jnp.where(line == 2 + i, wide, values)
    high, low = high_low(values)

    def down(count, shift):
        pick = hot((iota((count, DOM), 0) >> shift) == iota((count, DOM), 1))
        return (16.0 * nt(pick, high) + nt(pick, low)).astype(I32) - 1

    def along(count, shift):
        pick = hot((iota((DOM, count), 1) >> shift) == iota((DOM, count), 0))
        return (16.0 * nn(high, pick) + nn(low, pick)).astype(I32) - 1

    by_row = down(NODE, 3)
    m = iota((NODE, 1), 0)
    j = m & 7
    first, second, hub0, hub1 = [by_row[:, k : k + 1] for k in range(4)]
    pick_sig = jnp.where(j == 0, first, jnp.where(j == 1, second, -1))
    pick_sig = jnp.where(j == 2, hub0, jnp.where(j == 3, hub1, pick_sig))
    two = 2 * (m >> 3) + (j & 1)
    not_mine = (m >> 6) != slot
    pick_ext = jnp.where((j >> 1) == 2, two, -1)
    pick_ext = jnp.where(((j >> 1) == 1) & not_mine, BLK + two, pick_ext)
    last = [
        jnp.where(j == 6, first, jnp.where(j == 7, hub1, -1)),
        jnp.where(j == 6, second, -1),
        jnp.where(j == 6, hub0, -1),
    ]
    by_hub = down(BLK, 1)
    odd = (iota((BLK, 1), 0) & 1) == 1
    hub_col = jnp.where(odd, by_hub[:, 3:4], by_hub[:, 2:3])
    lane = iota((NODE, BLK), 1)
    hub_wide = jnp.concatenate([hub_col, jnp.full((NODE - BLK, 1), -1, I32)], 0)
    cols_out[...] = jnp.where(
        lane == 0, pick_sig, jnp.where(lane == 1, pick_ext, jnp.where(lane == 2, hub_wide, -1))
    )
    flat = along(NODE, 3)
    mr = iota((1, NODE), 1)
    jr = mr & 7
    back_row = jnp.where(jr == 4, flat[0:1], jnp.where(jr == 5, flat[1:2], -1))
    flat_hub = along(BLK, 1)
    odd = (iota((1, BLK), 1) & 1) == 1
    hub_row = jnp.where(odd, flat_hub[3:4], flat_hub[2:3])
    hub_row = jnp.concatenate([hub_row, jnp.full((1, NODE - BLK), -1, I32)], 1)
    j16 = iota((HUB_PER, NODE), 0)
    at = iota((HUB_PER, NODE), 1)
    lay = hot((j16 == 2 * (at >> 3) + ((at >> 2) & 1)) & (at < DOM))
    hub_mine = (16.0 * nn(held_high, lay) + nn(held_low, lay)).astype(I32)[0:1] - 1
    line = iota((8, NODE), 0)
    rows_out[...] = jnp.where(
        line == 0, back_row, jnp.where(line == 2, hub_row, jnp.where(line == 3, hub_mine, -1))
    )

    add_tiles(acc, trow, tcol, tmask, tiles, 4)
    for r in range(4):
        for c in range(2):
            block = acc[c * 4 + r]
            far[c * BLK : (c + 1) * BLK, r * BLK : (r + 1) * BLK] = block.T.astype(BF)
    from_sig = pick_rows(pick_sig, NODE)
    from_ext = pick_rows(pick_ext, EXT - NODE)
    for t in range(T1):
        ext = nn(far[...], cot[t]).astype(BF)
        out = (
            nn(from_ext, ext)
            + nn(from_sig, sig[t])
            + nn(pick_rows(last[t], NODE), sig[HIST - 1])
        )
        send[:, t * C : (t + 1) * C] = out.astype(BF)


def own_kernel(
    trow, tcol, tmask, tiles, conv, sig, cot, a_out, a_hub, at_out, hid, fac_f, fac_g, mix0, acc
):
    add_tiles(acc, trow, tcol, tmask, tiles, 0)
    for r in range(4):
        for c in range(6):
            block = acc[c * 4 + r]
            a_out[r * BLK : (r + 1) * BLK, c * BLK : (c + 1) * BLK] = block.astype(BF)
            at_out[c * BLK : (c + 1) * BLK, r * BLK : (r + 1) * BLK] = block.T.astype(BF)
    a_hub[...] = a_out[:, NODE + BLK :]
    total = jnp.zeros((C, C), F32)
    weights = conv
    for t in range(T1):
        h, p, q = gates(sig[t], sig[t + 1], weights)
        hid[t] = h
        fac_f[t] = p
        fac_g[t] = q
        total += tn(h, cot[t])
    mix0[...] = total


def hub_blocks(recv, owner, with_last):
    row = iota((8, NODE), 0)
    m = iota((8, NODE), 1)
    which = row >> 2
    step = row & 3
    forward = jnp.zeros((8, C), F32)
    backward = jnp.zeros((8, C), F32)
    for c in range(T1):
        block = recv[:, c * C : (c + 1) * C]
        f = (step == c) & (m == owner * 8 + 2 + which)
        if with_last and c == 2:
            f = f | ((row == 3) & (m == owner * 8 + 6))
        if with_last and c == 0:
            f = f | ((row == 7) & (m == owner * 8 + 7))
        b = (step == c) & ((m & 7) == 2 + which) & ((m >> 3) != owner)
        forward += nn(hot(f), block)
        backward += nn(hot(b), block)
    return forward, backward


def hub_kernel(me, owners, recv, send):
    owner = owners[me[0] >> 3]
    forward, backward = hub_blocks(recv, owner, True)
    at_owner = iota((DOM, 8, C), 0) == owner
    send[...] = jnp.where(at_owner, backward[None], forward[None]).astype(BF)


def halo_kernel(
    recv, conv, cols, rows, at_mat, a_mat, hid, cot, sig, back, hop, sig_x, hub_sig
):
    r = iota((BLK, NODE), 0)
    m = iota((BLK, NODE), 1)
    base = (r >> 1) * 8
    odd = r & 1
    pick0 = hot(m == base + odd)
    pick3a = hot((odd == 0) & (m == base + 6))
    pick3b = hot((odd == 1) & (m == base + 6))
    blocks = [recv[:, t * C : (t + 1) * C] for t in range(T1)]
    weights = conv
    far = [nn(pick0, block).astype(BF) for block in blocks]
    far.append((nn(pick3a, blocks[0]) + nn(pick3b, blocks[1])).astype(BF))
    for t in range(HIST):
        sig_x[t] = far[t]
    hid_x = [gates(far[t], far[t + 1], weights)[0] for t in range(T1)]
    put_halo = put_rows(rows[0:1, :], NODE)
    put_hub_own = put_rows(rows[2:3, 0:BLK], NODE)
    for t in range(T1):
        hub = nn(at_mat[NODE + BLK :, :], cot[t]).astype(BF)
        back[t] = (
            nn(at_mat[:NODE, :], cot[t]) + nn(put_halo, blocks[t]) + nn(put_hub_own, hub)
        )
        hop[t] = nn(a_mat[:, :NODE], hid[t]) + nn(a_mat[:, NODE : NODE + BLK], hid_x[t])
    own_pick = pick_rows(cols[0:BLK, 2:3], NODE)
    for t in range(HIST):
        hub_sig[t] = nn(own_pick, sig[t]).astype(BF)


def rows_kernel(
    me, owners, recv, cols, rows, conv, hub0, hub1, a_hub, hop_part, back_part, at_mat,
    send, back_out, hop_out, ext_out, ext_hub, sig_x, pick_sig, pick_ext,
):
    t = pl.program_id(0)

    @pl.when(t == 0)
    def _():
        pick_sig[...] = pick_rows(cols[:, 0:1], NODE)
        pick_ext[...] = pick_rows(cols[:, 1:2], EXT - NODE)

    r = iota((BLK, NODE), 0)
    m = iota((BLK, NODE), 1)
    base = (r >> 1) * 8 + (r & 1) * 4
    own_node = cols[0:BLK, 2:3]
    hubs = recv[...]
    far = []
    for s, hub_sig in ((0, hub0), (1, hub1)):
        hub_pick = hot((m == base + (t + s)) & (own_node < 0))
        far.append((nn(hub_pick, hubs) + hub_sig[0].astype(F32)).astype(BF))
        sig_x[t + s] = far[s]
    mine, target = own_hub_block(me, owners, rows, recv)
    h = gates(far[0], far[1], conv)[0]
    hop = (hop_part[0] + nn(a_hub[...], h)).astype(BF)
    hop_out[0] = hop
    back = (back_part[0] + nn(put_step(target, t), mine)).astype(BF)
    back_out[0] = back
    ext = nn(at_mat[...], back).astype(BF)
    out = nn(pick_sig[...], hop) + nn(pick_ext[...], ext[NODE:])
    send[...] = out.astype(BF)
    ext_out[0] = ext
    ext_hub[0] = ext[NODE + BLK :]


def weight_kernel(
    core, conv, mix, hop, cot, back, ext, sig0, sig1, halo0, halo1, hub0, hub1, fac_f, fac_g,
    mix0, keep, give, acc,
):
    t = pl.program_id(0)

    @pl.when(t == 0)
    def _():
        acc[...] = jnp.zeros_like(acc)

    acc[4] += tn(hop[0], cot[0])
    acc[5] += tn(hop[0], back[0])
    through = nt(ext[0], mix[2])
    gh = nt(cot[0], mix[0]) + nt(back[0], mix[1]) + through[:NODE]
    far_sig = (
        jnp.concatenate([halo0[0], hub0[0]], 0),
        jnp.concatenate([halo1[0], hub1[0]], 0),
    )
    _, p, q = gates(far_sig[0], far_sig[1], conv)
    own = ((gh * fac_f[0]).astype(BF), (gh * fac_g[0]).astype(BF))
    far = ((through[NODE:] * p).astype(BF), (through[NODE:] * q).astype(BF))
    for s, sig in ((0, sig0), (1, sig1)):
        for k in range(2):
            acc[2 * k + s] += tn(sig[0], own[k]) + tn(far_sig[s], far[k])

    @pl.when(t == T1 - 1)
    def _():
        first = core[0] == 0
        mats = (acc[0], acc[1], acc[2], acc[3], mix0[...], acc[4], acc[5])
        pieces = [x[:, s * BLK : (s + 1) * BLK] for x in mats for s in range(2)]
        for j in range(PIECES):
            low, high = pieces[j], pieces[PIECES + j]
            give[j * C : (j + 1) * C, :] = jnp.where(first, high, low)
            keep[j * C : (j + 1) * C, :] = jnp.where(first, low, high)


def pair_kernel(batch, keep, got, *outs):
    mine, other = keep, got
    for k in range(BATCH):
        at = pl.ds(pl.multiple_of(((batch[0] + k) & (BATCH - 1)) * CHUNK, DOM), CHUNK)
        outs[k][...] = (mine[at, :] + other[at, :]).astype(BF)


def same_slot(n, m):
    return (n == (m >> 3) * PIECES + (m & 7)) & ((m & 7) < PIECES)


def second_hub_kernel(me, owners, recv, part0, part1, part2, part3, send):
    owner = owners[me[0] >> 3]
    forward, backward = hub_blocks(recv, owner, False)
    total = part0[...].astype(F32) + part1[...].astype(F32)
    total += part2[...].astype(F32) + part3[...].astype(F32)
    at_owner = iota((DOM, 8, C), 0) == owner
    send[:, :, 0:C] = jnp.where(at_owner, backward[None], forward[None]).astype(BF)
    place = hot(same_slot(iota((NODE, CHUNK), 1), iota((NODE, CHUNK), 0)))
    send[:, :, C:] = nn(place, total.astype(BF)).astype(BF).reshape(DOM, 8, BLK)


def spread_kernel(recv, send):
    even = jnp.zeros((8, BLK), F32)
    odd = jnp.zeros((8, BLK), F32)
    for p in range(0, DOM, 2):
        even += recv[p, :, C:].astype(F32)
        odd += recv[p + 1, :, C:].astype(F32)
    is_odd = (iota((DOM, 8, BLK), 0) & 1) == 1
    send[...] = jnp.where(is_odd, odd[None], even[None]).astype(BF)


def near_kernel(
    recv, cols, rows, a_mat, mix, hop_ref, hid, sig, ext_hub, ext, back_ref, cot,
    mixed, two, gh_out, hop_hub,
):
    r = iota((BLK, NODE), 0)
    m = iota((BLK, NODE), 1)
    pick0 = hot(m == (r >> 1) * 8 + (r & 1))
    own_pick = pick_rows(cols[0:BLK, 2:3], NODE)
    put_halo = put_rows(rows[0:1, :], NODE)
    put_hub_own = put_rows(rows[2:3, 0:BLK], NODE)
    for t in range(T1):
        block = recv[:, t * C : (t + 1) * C]
        hop = hop_ref[t]
        rows_halo = nn(pick0, block).astype(BF)
        two[t] = nn(a_mat[:, :NODE], hop) + nn(a_mat[:, NODE : NODE + BLK], rows_halo)
        hop_hub[t] = nn(own_pick, hop).astype(BF)
        mixed[t] = sig[t + 1].astype(F32) + nn(hid[t], mix[0]) + nn(hop, mix[1])
        back = (nn(put_halo, block) + nn(put_hub_own, ext_hub[t])).astype(BF)
        own = nt(cot[t], mix[0]) + nt(back_ref[t], mix[1]) + nt(ext[t, 0:NODE, :], mix[2])
        gh_out[t] = own + nt(back, mix[2])


def signal_kernel(
    me, owners, recv, rows, mix, conv, gh_ref, fac_f, fac_g, cot, sgrad, carried
):
    t = pl.program_id(0)

    @pl.when(t == 0)
    def _():
        carried[...] = jnp.zeros_like(carried)

    mine, target = own_hub_block(me, owners, rows, recv)
    back = nn(put_step(target, t), mine).astype(BF)
    gh = gh_ref[0] + nt(back, mix[2])
    gf = (gh * fac_f[0]).astype(BF)
    gg = (gh * fac_g[0]).astype(BF)
    early = nt(gf, conv[0, 0]) + nt(gg, conv[1, 0])
    late = nt(gf, conv[0, 1]) + nt(gg, conv[1, 1]) + cot[0].astype(F32)
    sgrad[t] = (early + carried[...]).astype(BF)
    carried[...] = late

    @pl.when(t == T1 - 1)
    def _():
        sgrad[T1] = late.astype(BF)


def layer_kernel(recv, cols, a_hub, mix, hop_hub, mixed, two_ref, layer):
    r = iota((BLK, NODE), 0)
    m = iota((BLK, NODE), 1)
    base = (r >> 1) * 8 + (r & 1) * 4
    own_node = cols[0:BLK, 2:3]
    hubs = recv[:, 0:C]
    for t in range(T1):
        hub_pick = hot((m == base + t) & (own_node < 0))
        rows_hub = (nn(hub_pick, hubs) + hop_hub[t].astype(F32)).astype(BF)
        two = (two_ref[t] + nn(a_hub[...], rows_hub)).astype(BF)
        layer[t] = (mixed[t] + nn(two, mix[2])).astype(BF)


def tie_kernel(chunk, kept, chunk_out, kept_out):
    del kept, kept_out
    pack = hot(same_slot(iota((CHUNK, NODE), 0), iota((CHUNK, NODE), 1)))
    chunk_out[...] = nn(pack, chunk[...]).astype(BF)


def scale_kernel(core, batch, *refs):
    mine, other = refs[0:BATCH], refs[BATCH : 2 * BATCH]
    conv_grad, mix_grad, held = refs[2 * BATCH :]
    factor = 1.0 / math.sqrt(NODE * DOM * BATCH * T1)
    first = core[0] == 0
    for k in range(BATCH):
        block = (batch[0] + BATCH - k) & (BATCH - 1)
        at = pl.ds(pl.multiple_of(block * CHUNK, DOM), CHUNK)
        held[0, at, :] = jnp.where(first, mine[k][...], other[k][...])
        held[1, at, :] = jnp.where(first, other[k][...], mine[k][...])
    for p in range(2 * PIECES):
        j = p % PIECES
        piece = held[p // PIECES, j * C : (j + 1) * C, :].astype(F32) * factor
        lanes = slice((p % 2) * BLK, (p % 2 + 1) * BLK)
        if p < 8:
            conv_grad[p // 2, :, lanes] = piece
        else:
            mix_grad[p // 2 - 4, :, lanes] = piece


def swap(x, axis):
    return lax.all_to_all(x, axis, split_axis=0, concat_axis=0, tiled=True)


def body(
    signal,
    cotangent,
    conv,
    mix,
    send_rows,
    send_mask,
    tile_vals,
    tile_row,
    tile_col,
    tile_mask,
    hub_owner,
    hub_rows,
):
    me = lax.axis_index("dom").astype(I32)
    core = (me & 1).reshape(1)
    me = me.reshape(1)
    batch = lax.axis_index("batch").astype(I32).reshape(1)
    sig = jnp.transpose(signal[:, 0], (1, 0, 2))
    cot = jnp.transpose(cotangent[:, 0], (1, 0, 2))

    field = (T1, NODE, C)
    edge = (T1, BLK, C)
    edge4 = (HIST, BLK, C)
    half = (PIECES * C, BLK)
    chunk = (CHUNK, BLK)
    cols, rows, send1 = call(
        start_kernel,
        [((NODE, BLK), I32), ((8, NODE), I32), ((NODE, EXT), BF)],
        (tile_row, tile_col, tile_mask, me, hub_owner, tile_vals, send_rows.T, send_mask.T,
         hub_rows, cot, sig),
        smem=5,
        scratch=[pltpu.VMEM((8, BLK, BLK), F32), pltpu.VMEM((EXT - NODE, NODE), BF)],
        flops=2 << 30,
    )
    recv1 = swap(send1.reshape(DOM, 8, EXT), "dom").reshape(NODE, EXT)
    a_mat, a_hub, at_mat, hid, fac_f, fac_g, mix0 = call(
        own_kernel,
        [((NODE, EXT), BF), ((NODE, BLK), BF), ((EXT, NODE), BF), (field, BF), (field, F32),
         (field, F32), ((C, C), F32)],
        (tile_row, tile_col, tile_mask, tile_vals, conv, sig, cot),
        smem=3,
        scratch=[pltpu.VMEM((24, BLK, BLK), F32)],
        flops=8 << 30,
    )
    (send2,) = call(
        hub_kernel, [((DOM, 8, C), BF)], (me, hub_owner, recv1), 8, smem=2, flops=1 << 28
    )
    recv2 = swap(send2, "dom").reshape(NODE, C)
    back_part, hop_part, sig_h, hub_sig = call(
        halo_kernel,
        [(field, F32), (field, F32), (edge4, BF), (edge4, BF)],
        (recv1, conv, cols, rows, at_mat, a_mat, hid, cot, sig),
        flops=8 << 30,
    )
    send3, back, hop, ext, ext_hub, sig_u = stepped(
        rows_kernel,
        [((NODE, EXT), BF), (field, BF), (field, BF), ((T1, EXT, C), BF), (edge, BF),
         (edge4, BF)],
        (me, hub_owner, recv2, cols, rows, conv, hub_sig, hub_sig, a_hub, hop_part, back_part,
         at_mat),
        ("all", "all", "all", "all", "this", "next", "all", "this", "this", "all"),
        ("lanes", "this", "this", "this", "this", "all"),
        smem=2,
        scratch=[pltpu.VMEM((NODE, NODE), BF), pltpu.VMEM((NODE, EXT - NODE), BF)],
        flops=4 << 30,
    )
    recv3 = swap(send3.reshape(DOM, 8, EXT), "dom").reshape(NODE, EXT)
    keep, give = stepped(
        weight_kernel,
        [(half, F32), (half, F32)],
        (core, conv, mix, hop, cot, back, ext, sig, sig, sig_h, sig_h, sig_u, sig_u, fac_f, fac_g,
         mix0),
        ("all", "all", "this", "this", "this", "this", "this", "next", "this", "next", "this",
         "next", "this", "this", "all"),
        ("all", "all"),
        smem=1,
        scratch=[pltpu.VMEM((6, C, C), F32)],
        flops=8 << 30,
    )
    pairs = [(i, i ^ 1) for i in range(DOM)]
    rounds = [[(i, (i + k) % BATCH) for i in range(BATCH)] for k in range(BATCH)]
    got = lax.ppermute(give, "dom", pairs)
    parts = call(
        pair_kernel, [(chunk, BF)] * BATCH, (batch, keep, got), 8, smem=1, flops=1 << 26
    )
    parts = [parts[0]] + [
        lax.ppermute(parts[k], "batch", rounds[k]) for k in range(1, BATCH)
    ]
    (send4,) = call(
        second_hub_kernel,
        [((DOM, 8, C + BLK), BF)],
        (me, hub_owner, recv3, *parts),
        8,
        smem=2,
        flops=1 << 28,
    )
    recv4 = swap(send4, "dom")
    mixed, two, gh, hop_hub = call(
        near_kernel,
        [(field, F32), (field, F32), (field, F32), (edge, BF)],
        (recv3, cols, rows, a_mat, mix, hop, hid, sig, ext_hub, ext, back, cot),
        flops=8 << 30,
    )
    recv4, mixed, two, gh, hop_hub = lax.optimization_barrier((recv4, mixed, two, gh, hop_hub))
    (send5,) = call(spread_kernel, [((DOM, 8, BLK), BF)], (recv4,), 6, flops=1 << 26)
    recv5 = swap(send5, "dom").reshape(NODE, BLK)
    recv4 = recv4.reshape(NODE, C + BLK)
    (sgrad,) = stepped(
        signal_kernel,
        [((HIST, NODE, C), BF)],
        (me, hub_owner, recv4, rows, mix, conv, gh, fac_f, fac_g, cot),
        ("all", "all", "all", "all", "this", "this", "this", "this"),
        ("all",),
        smem=2,
        scratch=[pltpu.VMEM((NODE, C), F32)],
        flops=8 << 30,
    )
    sgrad = jnp.transpose(sgrad, (1, 0, 2))
    vmem, keep_place = (pl.BlockSpec(memory_space=m) for m in (pltpu.VMEM, pl.ANY))
    recv5, sgrad = pl.pallas_call(
        tie_kernel,
        out_shape=[jax.ShapeDtypeStruct(x, BF) for x in (chunk, sgrad.shape)],
        in_specs=[vmem, keep_place],
        out_specs=[vmem, keep_place],
        input_output_aliases={1: 1},
        compiler_params=pltpu.CompilerParams(vmem_limit_bytes=4 << 20),
    )(recv5, sgrad)
    first_swap = lax.ppermute(recv5, "dom", pairs)
    mine = [recv5] + [lax.ppermute(recv5, "batch", rounds[k]) for k in range(1, BATCH)]
    (layer,) = call(
        layer_kernel,
        [(field, BF)],
        (recv4, cols, a_hub, mix, hop_hub, mixed, two),
        flops=4 << 30,
    )
    mine, layer = lax.optimization_barrier((mine, layer))
    other = [first_swap] + [lax.ppermute(one, "dom", pairs) for one in mine[1:]]
    conv_grad, mix_grad = call(
        scale_kernel,
        [((4, C, C), F32), ((3, C, C), F32)],
        (core, batch, *mine, *other),
        10,
        smem=2,
        scratch=[pltpu.VMEM((2, PIECES * C, BLK), BF)],
        flops=1 << 20,
    )
    layer = jnp.transpose(layer, (1, 0, 2))[:, None]
    return layer, sgrad[:, None], conv_grad.reshape(2, 2, C, C), mix_grad


def solution(mesh):
    placed = (
        P("dom", "batch", None, None),
        P("dom", "batch", None, None),
        P(),
        P(),
        P("dom", None),
        P("dom", None),
        P("dom", None, None),
        P("dom"),
        P("dom"),
        P("dom"),
        P(),
        P(),
    )
    return jax.shard_map(
        body,
        mesh=mesh,
        in_specs=placed,
        out_specs=(P("dom", "batch", None, None), P("dom", "batch", None, None), P(), P()),
        check_vma=False,
    )
```
